512 devices in a mesh: lon: 64 (over z, y_hi, core), lat: 8 (over x, y_lo).
Axes of the slice: x: 4, y: 4 (y_hi: 2, y_lo: 2; y = y_hi * 2 + y_lo), z: 16, core: 2. Of those that a mesh axis runs over, the one named last changes fastest.
Arguments:
- field: float32 [2, 2048, 2048], P(None, 'lon', 'lat'), may hold values from -6 to 6
- offsets: int32 [2048], P('lat'), may hold values from 0 to 2047, as said below
- fraction: float32 [2048], P('lat'), may hold values from 0 to 1
- helm: float32 [2], replicated, may hold values from 4 to 32
Outputs:
- solution: float32 [2, 2048, 2048], P(None, 'lon', 'lat')
The draws below stay inside these ranges and needn't reach their ends.
Inputs may be any that keep to these rules, and one draw needn't show every extreme that they name: `offsets`: each row's offset is a whole number of longitude points; some row needs the whole circle but one point, some row none.
All inputs are finite; a program needn't handle non-finite values.
Results may differ from the reference program's by a relative error of at most 0.00002.
Values sent between devices are 32-bit elements; how exact they have to be, the bound alone decides.
A program may use at most 64 MiB of HBM per device.

```python
import math
import jax
import jax.numpy as jnp
from jax import lax

LEV = 2
LON_DEV = 32
SMOOTH = 2
COARSE = 4
NLON = 2048
NLAT = 2048


def draw_offsets(key, part):
    first, second = jax.random.split(jax.random.fold_in(key, 17))
    remain = jax.random.randint(first, (NLAT,), 0, LON_DEV)
    blocks = jax.random.randint(second, (NLAT,), 0, NLON // LON_DEV)
    row = jnp.arange(NLAT)
    polar = (row < NLAT // 6) | (row >= NLAT - NLAT // 6)
    offset = remain + jnp.where(polar, blocks * LON_DEV, 0)
    offset = offset.at[0].set(NLON - 1)
    offset = offset.at[NLAT // 2].set(0)
    return offset.astype(jnp.int32)


def draw_field(key, part):
    keys = jax.random.split(jax.random.fold_in(key, 29), 5)
    lon = jnp.arange(NLON, dtype=jnp.float32)[None, :, None] / NLON
    lat = (jnp.arange(NLAT, dtype=jnp.float32)[None, None, :] + 0.5) / NLAT
    wave_lon = jax.random.randint(keys[0], (LEV, 1, 1), 1, 4).astype(jnp.float32)
    wave_lat = jax.random.randint(keys[1], (LEV, 1, 1), 1, 4).astype(jnp.float32)
    phase_lon = jax.random.uniform(keys[2], (LEV, 1, 1), jnp.float32, 0.0, 2.0 * math.pi)
    phase_lat = jax.random.uniform(keys[3], (LEV, 1, 1), jnp.float32, 0.0, 2.0 * math.pi)
    zonal = jnp.cos(2.0 * math.pi * wave_lon * lon + phase_lon)
    meridional = jnp.cos(math.pi * wave_lat * lat + phase_lat)
    noise = jnp.clip(jax.random.normal(keys[4], (LEV, NLON, NLAT), jnp.float32), -3.0, 3.0)
    values = 1.5 * zonal + 1.5 * meridional + noise
    return values.astype(jnp.float32)


def level_of(stream_key, dims, shards, smallest, top_value):
    gain = 1.0
    for dim, shards_of in shards:
        heights = jax.random.uniform(jax.random.fold_in(jax.random.fold_in(stream_key, 6), dim), (shards_of,), jnp.float32, smallest / len(shards), top_value / len(shards))
        gain = gain * jnp.repeat(jnp.exp(heights), dims[dim] // shards_of).reshape((-1,) + (1,) * (len(dims) - 1 - dim))
    return gain


def setup_inputs(seed: int = 0) -> dict:
    streams_of = jax.random.split(jax.random.key(seed), 5)
    field = draw_field(jax.random.fold_in(streams_of[4], 71), 0)
    offsets = draw_offsets(jax.random.fold_in(streams_of[4], 71), 0)
    fraction = jnp.clip(1.0 * jax.random.uniform(streams_of[2], (NLAT,), jnp.float32) ** level_of(streams_of[2], (NLAT,), ((0, 8),), -0.2, 0.2), 0.0, 1.0)
    helm = jnp.clip(jnp.exp(jax.random.uniform(streams_of[3], (LEV,), jnp.float32, math.log(4.0), math.log(32.0))), 4.0, 32.0)
    return dict(field=field, offsets=offsets, fraction=fraction, helm=helm)


OMEGA = 0.8


def pair_sum(x):
    zonal = jnp.roll(x, 1, axis=1) + jnp.roll(x, -1, axis=1)
    padded = jnp.pad(x, ((0, 0), (0, 0), (1, 1)))
    return zonal + padded[:, :, 2:] + padded[:, :, :-2]


def relax(x, rhs, coef):
    diag = 1.0 + 4.0 * coef
    applied = diag * x - coef * pair_sum(x)
    return x + OMEGA * (rhs - applied) / diag


def defect(x, rhs, coef):
    diag = 1.0 + 4.0 * coef
    return rhs - (diag * x - coef * pair_sum(x))


def restrict(x):
    lev, nlon, nlat = x.shape
    return x.reshape(lev, nlon // 2, 2, nlat // 2, 2).mean(axis=(2, 4))


def prolong(x):
    return jnp.repeat(jnp.repeat(x, 2, axis=1), 2, axis=2)


def reference(field, offsets, fraction, helm):
    column = jnp.arange(NLON, dtype=jnp.int32)
    index = ((column[:, None] - offsets[None, :]) % NLON).astype(jnp.int32)
    shifted = lax.map(lambda level: jnp.take_along_axis(level, index, axis=0), field)
    s = fraction[None, None, :]
    w_one = -s * (s - 1.0) * (s - 2.0) / 6.0
    w_two = (s + 1.0) * (s - 1.0) * (s - 2.0) / 2.0
    w_three = -(s + 1.0) * s * (s - 2.0) / 2.0
    w_four = (s + 1.0) * s * (s - 1.0) / 6.0
    departure = (w_one * jnp.roll(shifted, -1, axis=1) + w_two * shifted
                 + w_three * jnp.roll(shifted, 1, axis=1) + w_four * jnp.roll(shifted, 2, axis=1))
    coef0 = helm[:, None, None]
    coef1 = coef0 / 4.0
    coef2 = coef0 / 16.0
    level0 = jnp.zeros_like(departure)
    for sweep in range(SMOOTH):
        level0 = relax(level0, departure, coef0)
    rhs1 = restrict(defect(level0, departure, coef0))
    level1 = jnp.zeros_like(rhs1)
    for sweep in range(SMOOTH):
        level1 = relax(level1, rhs1, coef1)
    rhs2 = restrict(defect(level1, rhs1, coef1))
    level2 = jnp.zeros_like(rhs2)
    for sweep in range(COARSE):
        level2 = relax(level2, rhs2, coef2)
    level1 = level1 + prolong(level2)
    for sweep in range(SMOOTH):
        level1 = relax(level1, rhs1, coef1)
    level0 = level0 + prolong(level1)
    for sweep in range(SMOOTH):
        level0 = relax(level0, departure, coef0)
    return level0
```

```python
import jax
import jax.numpy as jnp
from jax import lax
from jax.experimental import pallas as pl
from jax.experimental.pallas import tpu as pltpu
from jax.sharding import PartitionSpec as P

MESH = pl.DeviceIdType.MESH
NLONDEV = 64
NLATDEV = 8
LANES = 128


def roll(x, shift):
    return pltpu.roll(x, shift % LANES, 1)


def lane_iota(rows):
    return lax.broadcasted_iota(jnp.int32, (rows, LANES), 1)


def sub_iota():
    return lax.broadcasted_iota(jnp.int32, (8, LANES), 0)


def pack_field(half):
    low = lane_iota(16) < 64
    pieces = []
    for chunk in range(4):
        for lev in range(2):
            first, second = half(lev, 0, chunk // 2), half(lev, 1, chunk // 2)
            if chunk % 2 == 0:
                pieces.append(jnp.where(low, first, roll(second, 64)))
            else:
                pieces.append(jnp.where(low, roll(first, 64), second))
    return jnp.concatenate(pieces, axis=0)


def by_chunk(values, dtype):
    chunk = sub_iota() // 2
    full = jnp.full((8, LANES), values[0], dtype)
    for c in range(1, 4):
        full = jnp.where(chunk == c, jnp.full((8, LANES), values[c], dtype), full)
    return full


def shift_rows(v, offset):
    coarse, fine = offset // 16, offset % 16
    for bit in range(7):
        take = (coarse // (1 << bit)) % 2 == 1
        v = [jnp.where(take, roll(x, 1 << bit), x) for x in v]
    for bit in range(4):
        by = 1 << bit
        take = (fine // by) % 2 == 1
        v = [jnp.where(take, v[r - by] if r >= by else roll(v[r - by + 16], 1), v[r]) for r in range(16)]
    return v


def interpolate(g, s):
    w_one = -s * (s - 1.0) * (s - 2.0) / 6.0
    w_two = (s + 1.0) * (s - 1.0) * (s - 2.0) / 2.0
    w_three = -(s + 1.0) * s * (s - 2.0) / 2.0
    w_four = (s + 1.0) * s * (s - 1.0) / 6.0
    ext = [roll(g[14], 1), roll(g[15], 1)] + g + [roll(g[0], -1)]
    return [w_one * ext[r + 3] + w_two * ext[r + 2] + w_three * ext[r + 1] + w_four * ext[r] for r in range(16)]


def exchange_kernel(field, offsets, fraction, ext, send1, recv1, send2, recv2, work,
                    sems, near_send, near_recv):
    d = lax.axis_index("lon")
    g = lax.axis_index("lat")
    north, south = g > 0, g < NLATDEV - 1

    barrier = pltpu.get_barrier_semaphore()

    def greet(j, carry):
        pl.semaphore_signal(barrier, inc=1, device_id={"lon": lax.rem(d + j, NLONDEV)}, device_id_type=MESH)
        return carry

    lax.fori_loop(1, NLONDEV, greet, 0)
    for there, to in ((north, -1), (south, 1)):
        @pl.when(there)
        def _():
            for dd in (-1, 0, 1):
                pl.semaphore_signal(
                    barrier, inc=1,
                    device_id={"lon": lax.rem(d + dd + NLONDEV, NLONDEV), "lat": g + to},
                    device_id_type=MESH)

    packed = pack_field(lambda lev, hi, pair: field[lev, 16 * hi:16 * hi + 16, 128 * pair:128 * pair + 128]).T
    for hi in range(2):
        send1[pl.ds(hi, 64, stride=2), :] = packed[64 * hi:64 * hi + 64]

    pl.semaphore_wait(barrier, NLONDEV - 1 + 3 * (north.astype(jnp.int32) + south.astype(jnp.int32)))

    def all_to_all(src, dst, which):
        mine = pl.ds(2 * d, 2)

        def send(j, carry):
            step = jnp.where(j % 2 == 0, 32 + j // 2, 31 - j // 2)
            peer = lax.rem(d + step, NLONDEV)
            pltpu.make_async_remote_copy(
                src_ref=src.at[pl.ds(2 * peer, 2)],
                dst_ref=dst.at[mine],
                send_sem=sems.at[2 * which],
                recv_sem=sems.at[2 * which + 1],
                device_id={"lon": peer},
                device_id_type=MESH,
            ).start()
            return carry

        lax.fori_loop(0, NLONDEV - 1, send, 0)
        pltpu.make_async_copy(src.at[mine], dst.at[mine], sems.at[2 * which + 1]).start()
        pltpu.make_async_copy(dst, dst, sems.at[2 * which + 1]).wait()

    def sent(src, which):
        part = src.at[pl.ds(0, 2 * NLONDEV - 2)]
        pltpu.make_async_copy(part, part, sems.at[2 * which]).wait()

    all_to_all(send1, recv1, 0)
    work[...] = recv1[...].T
    v = [work[pl.ds(r, 8, stride=16), :] for r in range(16)]
    own = [d + 64 * c for c in range(4)]
    v = shift_rows(v, by_chunk([offsets[i] for i in own], jnp.int32))
    v = interpolate(v, by_chunk([fraction[i] for i in own], jnp.float32))
    for r in range(16):
        work[pl.ds(r, 8, stride=16), :] = v[r]
    send2[...] = work[...].T
    all_to_all(send2, recv2, 1)
    ext[1, 32:160, :] = jnp.concatenate([recv2[pl.ds(hi, 64, stride=2), :] for hi in range(2)], axis=0).T

    def near(dd, to):
        if to == 0:
            src, dst = ext.at[1, pl.ds(32, 128)], ext.at[1 - dd, pl.ds(32, 128)]
        elif to < 0:
            src, dst = ext.at[1, pl.ds(32, 32)], ext.at[1 - dd, pl.ds(160, 32)]
        else:
            src, dst = ext.at[1, pl.ds(128, 32)], ext.at[1 - dd, pl.ds(0, 32)]
        return pltpu.make_async_remote_copy(
            src_ref=src, dst_ref=dst,
            send_sem=near_send.at[to + 1, dd + 1], recv_sem=near_recv.at[to + 1, dd + 1],
            device_id={"lon": lax.rem(d + dd + NLONDEV, NLONDEV), "lat": g + to},
            device_id_type=MESH)

    for dd in (-1, 1):
        near(dd, 0).start()
    for there, to in ((north, -1), (south, 1)):
        @pl.when(there)
        def _():
            for dd in (-1, 0, 1):
                near(dd, to).start()
    for edge, at in ((north, 0), (south, 160)):
        @pl.when(jnp.logical_not(edge))
        def _():
            for k in range(3):
                ext[k, at:at + 32, :] = jnp.zeros((32, LANES), jnp.float32)
    sent(send1, 0)
    sent(send2, 1)
    for dd in (-1, 1):
        near(dd, 0).wait()
    for there, to in ((north, -1), (south, 1)):
        @pl.when(there)
        def _():
            for dd in (-1, 0, 1):
                near(dd, to).wait_send()
                near(dd, -to).wait_recv()


def memo(f):
    seen = {}

    def g(i):
        if i not in seen:
            seen[i] = f(i)
        return seen[i]

    return g


def v_cycle(load, c0, inside):
    lane = lane_iota(8)

    def coefs(c):
        diag = 1.0 + 4.0 * c
        beta = inside * (0.8 / diag)
        return diag, c * inside, beta, beta * c

    diag0, mult0, beta0, gamma0 = coefs(c0)
    diag1, mult1, beta1, gamma1 = coefs(c0 * 0.25)
    diag2, mult2, beta2, gamma2 = coefs(c0 * 0.0625)

    def pairs(x, step):
        def f(i):
            return (x(i - 1) + x(i + 1)) + (roll(x(i), step) + roll(x(i), -step))
        return f

    def second(first, gamma, step):
        s = pairs(first, step)
        return memo(lambda i: 1.2 * first(i) + gamma * s(i))

    def sweep(x, first, gamma, step):
        s = pairs(x, step)
        return memo(lambda i: (0.2 * x(i) + first(i)) + gamma * s(i))

    def defect(x, rhs, diag, mult, step):
        s = pairs(x, step)
        return memo(lambda i: (rhs(i) - diag * x(i)) + mult * s(i))

    def restrict(x, step):
        even = (lane // step) % 2 == 0

        def f(i):
            q = x(2 * i) + x(2 * i + 1)
            return 0.25 * (q + jnp.where(even, roll(q, -step), roll(q, step)))
        return memo(f)

    dep = memo(load)
    first0 = memo(lambda i: beta0 * dep(i))
    x0 = second(first0, gamma0, 1)
    rhs1 = restrict(defect(x0, dep, diag0, mult0, 1), 1)
    first1 = memo(lambda i: beta1 * rhs1(i))
    x1 = second(first1, gamma1, 2)
    rhs2 = restrict(defect(x1, rhs1, diag1, mult1, 2), 2)
    first2 = memo(lambda i: beta2 * rhs2(i))
    x2 = second(first2, gamma2, 4)
    x2 = sweep(x2, first2, gamma2, 4)
    x2 = sweep(x2, first2, gamma2, 4)
    y1 = memo(lambda i: x1(i) + x2(i >> 1))
    y1 = sweep(y1, first1, gamma1, 2)
    y1 = sweep(y1, first1, gamma1, 2)
    y0 = memo(lambda i: x0(i) + y1(i >> 1))
    y0 = sweep(y0, first0, gamma0, 1)
    return sweep(y0, first0, gamma0, 1)


def window(rows):
    lane = lane_iota(8)

    def load(i):
        k, hi, r = (i + 32) // 32, (i % 32) // 16, i % 16
        before, here, after = rows(k, r), rows(k, r + 32), rows(k, r + 64)
        if hi == 0:
            sides = roll(jnp.where(lane < 32, after, before), -32)
            return jnp.where((lane >= 32) & (lane < 96), roll(here, 32), sides)
        sides = roll(jnp.where(lane < 96, after, before), 32)
        return jnp.where((lane >= 32) & (lane < 96), roll(here, -32), sides)

    return load


def inside_of(g):
    chunk, lane = sub_iota() // 2, lane_iota(8)
    out = ((g == 0) & (chunk == 0) & (lane < 32)) | ((g == NLATDEV - 1) & (chunk == 3) & (lane >= 96))
    return jnp.where(out, 0.0, 1.0)


def cycle_kernel(ext, helm, out, rows):
    g = lax.axis_index("lat")
    lev = sub_iota() % 2
    c0 = jnp.where(lev == 0, jnp.full((8, LANES), helm[0], jnp.float32), jnp.full((8, LANES), helm[1], jnp.float32))
    result = v_cycle(window(lambda k, at: ext[k, pl.ds(at, 8, stride=16), :]), c0, inside_of(g))
    for i in range(32):
        rows[8 * i:8 * i + 8, :] = result(i)
    low = lane_iota(8) < 64
    for block in range(4):
        for lev in range(2):
            for pair in range(2):
                left = rows[pl.ds(64 * block + 4 * pair + lev, 8, stride=8), :]
                right = rows[pl.ds(64 * block + 4 * pair + 2 + lev, 8, stride=8), :]
                out[lev, 8 * block:8 * block + 8, 128 * pair:128 * pair + 128] = jnp.where(
                    low, roll(left, -32), roll(right, 32))


def per_device(field, offsets, fraction, helm):
    vmem = pl.BlockSpec(memory_space=pltpu.VMEM)
    smem = pl.BlockSpec(memory_space=pltpu.SMEM)
    square = pltpu.VMEM((LANES, LANES), jnp.float32)
    ext = pl.pallas_call(
        exchange_kernel,
        out_shape=jax.ShapeDtypeStruct((3, 192, LANES), jnp.float32),
        in_specs=[vmem, smem, smem],
        out_specs=vmem,
        scratch_shapes=[
            square, square, square, square, square,
            pltpu.SemaphoreType.DMA((4,)),
            pltpu.SemaphoreType.DMA((3, 3)),
            pltpu.SemaphoreType.DMA((3, 3)),
        ],
        compiler_params=pltpu.CompilerParams(collective_id=0, has_side_effects=True, vmem_limit_bytes=16 * 1024 * 1024),
    )(field, offsets, fraction)
    return pl.pallas_call(
        cycle_kernel,
        out_shape=jax.ShapeDtypeStruct(field.shape, jnp.float32),
        in_specs=[vmem, smem],
        out_specs=vmem,
        scratch_shapes=[pltpu.VMEM((256, LANES), jnp.float32)],
        compiler_params=pltpu.CompilerParams(vmem_limit_bytes=16 * 1024 * 1024),
    )(ext, helm)


def solution(mesh):
    return jax.shard_map(
        per_device,
        mesh=mesh,
        in_specs=(P(None, "lon", "lat"), P("lat"), P("lat"), P()),
        out_specs=P(None, "lon", "lat"),
        check_vma=False,
    )
```

```python
import jax
import jax.numpy as jnp
from jax import lax
from jax.experimental import pallas as pl
from jax.experimental.pallas import tpu as pltpu
from jax.sharding import PartitionSpec as P

MESH = pl.DeviceIdType.MESH
NLONDEV = 64
NLATDEV = 8
OWNERS = 32
REP = NLONDEV // OWNERS
LANES = 128


def roll(x, shift):
    return pltpu.roll(x, shift % LANES, 1)


def lane_iota(rows):
    return lax.broadcasted_iota(jnp.int32, (rows, LANES), 1)


def sub_iota():
    return lax.broadcasted_iota(jnp.int32, (8, LANES), 0)


def pack_field(half):
    low = lane_iota(16) < 64
    pieces = []
    for chunk in range(4):
        for lev in range(2):
            first, second = half(lev, 0, chunk // 2), half(lev, 1, chunk // 2)
            if chunk % 2 == 0:
                pieces.append(jnp.where(low, first, roll(second, 64)))
            else:
                pieces.append(jnp.where(low, roll(first, 64), second))
    return jnp.concatenate(pieces, axis=0)


def by_chunk(values, dtype):
    chunk = sub_iota() // 2
    full = jnp.full((8, LANES), values[0], dtype)
    for c in range(1, 4):
        full = jnp.where(chunk == c, jnp.full((8, LANES), values[c], dtype), full)
    return full


def shift_rows(v, offset):
    coarse, fine = offset // 16, offset % 16
    for bit in range(7):
        take = (coarse // (1 << bit)) % 2 == 1
        v = [jnp.where(take, roll(x, 1 << bit), x) for x in v]
    for bit in range(4):
        by = 1 << bit
        take = (fine // by) % 2 == 1
        v = [jnp.where(take, v[r - by] if r >= by else roll(v[r - by + 16], 1), v[r]) for r in range(16)]
    return v


def interpolate(g, s):
    w_one = -s * (s - 1.0) * (s - 2.0) / 6.0
    w_two = (s + 1.0) * (s - 1.0) * (s - 2.0) / 2.0
    w_three = -(s + 1.0) * s * (s - 2.0) / 2.0
    w_four = (s + 1.0) * s * (s - 1.0) / 6.0
    ext = [roll(g[14], 1), roll(g[15], 1)] + g + [roll(g[0], -1)]
    return [w_one * ext[r + 3] + w_two * ext[r + 2] + w_three * ext[r + 1] + w_four * ext[r] for r in range(16)]


def exchange_kernel(field_in, offsets_in, fraction_in, ext, field, offsets, fraction, send1, recv1, send2, recv2, work,
                    load_sems, sems, near_send, near_recv):
    d = lax.axis_index("lon")
    g = lax.axis_index("lat")
    north, south = g > 0, g < NLATDEV - 1
    owner = d < OWNERS

    loads = [pltpu.make_async_copy(src, dst, load_sems.at[i]) for i, (src, dst) in enumerate(
        ((field_in, field), (offsets_in, offsets), (fraction_in, fraction)))]
    for load in loads:
        load.start()

    barrier = pltpu.get_barrier_semaphore()

    for there, to in ((north, -1), (south, 1)):
        @pl.when(there)
        def _():
            for dd in (-1, 0, 1):
                pl.semaphore_signal(
                    barrier, inc=1,
                    device_id={"lon": lax.rem(d + dd + NLONDEV, NLONDEV), "lat": g + to},
                    device_id_type=MESH)

    @pl.when(owner)
    def _():
        def greet(j, carry):
            pl.semaphore_signal(barrier, inc=1, device_id={"lon": lax.rem(d + j, NLONDEV)}, device_id_type=MESH)
            return carry

        lax.fori_loop(1, NLONDEV, greet, 0)

    loads[0].wait()
    packed = pack_field(lambda lev, hi, pair: field[lev, 16 * hi:16 * hi + 16, 128 * pair:128 * pair + 128]).T
    for hi in range(2):
        for s in range(REP):
            at = 64 * hi + OWNERS * s
            send1[s, pl.ds(hi, OWNERS, stride=2), :] = packed[at:at + OWNERS]

    one = owner.astype(jnp.int32)
    pl.semaphore_wait(barrier, OWNERS - one + 3 * (north.astype(jnp.int32) + south.astype(jnp.int32)))
    mine = pl.ds(2 * d, 2)

    def collect(j, carry):
        to = lax.rem(d + j, OWNERS)
        pltpu.make_async_remote_copy(
            src_ref=send1.at[:, pl.ds(2 * to, 2)], dst_ref=recv1.at[:, mine],
            send_sem=sems.at[0], recv_sem=sems.at[1],
            device_id={"lon": to}, device_id_type=MESH,
        ).start()
        return carry

    lax.fori_loop(one, OWNERS, collect, 0)
    loads[1].wait()
    loads[2].wait()

    @pl.when(owner)
    def _():
        pltpu.make_async_copy(send1.at[:, mine], recv1.at[:, mine], sems.at[1]).start()
        pltpu.make_async_copy(recv1, recv1, sems.at[1]).wait()
        for s in range(REP):
            work[s] = recv1[s].T
            v = [work[s, pl.ds(r, 8, stride=16), :] for r in range(16)]
            own = [d + OWNERS * s + 64 * c for c in range(4)]
            v = shift_rows(v, by_chunk([offsets[i] for i in own], jnp.int32))
            v = interpolate(v, by_chunk([fraction[i] for i in own], jnp.float32))
            for r in range(16):
                work[s, pl.ds(r, 8, stride=16), :] = v[r]
            send2[s] = work[s].T

        def spread(j, carry):
            to = j - lax.rem(j, 4) + lax.rem(j + d, 4)

            @pl.when(to != d)
            def _():
                pltpu.make_async_remote_copy(
                    src_ref=send2.at[:, pl.ds(2 * to, 2)], dst_ref=recv2.at[:, mine],
                    send_sem=sems.at[2], recv_sem=sems.at[3],
                    device_id={"lon": to}, device_id_type=MESH,
                ).start()
            return carry

        lax.fori_loop(0, NLONDEV, spread, 0)
        pltpu.make_async_copy(send2.at[:, mine], recv2.at[:, mine], sems.at[3]).start()

    pltpu.make_async_copy(recv2, recv2, sems.at[3]).wait()
    ext[1, 32:160, :] = jnp.concatenate(
        [recv2[s, pl.ds(hi, OWNERS, stride=2), :] for hi in range(2) for s in range(REP)], axis=0).T

    def near(dd, to):
        if to == 0:
            src, dst = ext.at[1, pl.ds(32, 128)], ext.at[1 - dd, pl.ds(32, 128)]
        elif to < 0:
            src, dst = ext.at[1, pl.ds(32, 32)], ext.at[1 - dd, pl.ds(160, 32)]
        else:
            src, dst = ext.at[1, pl.ds(128, 32)], ext.at[1 - dd, pl.ds(0, 32)]
        return pltpu.make_async_remote_copy(
            src_ref=src, dst_ref=dst,
            send_sem=near_send.at[to + 1, dd + 1], recv_sem=near_recv.at[to + 1, dd + 1],
            device_id={"lon": lax.rem(d + dd + NLONDEV, NLONDEV), "lat": g + to},
            device_id_type=MESH)

    for dd in (-1, 1):
        near(dd, 0).start()
    for there, to in ((north, -1), (south, 1)):
        @pl.when(there)
        def _():
            for dd in (-1, 0, 1):
                near(dd, to).start()
    for edge, at in ((north, 0), (south, 160)):
        @pl.when(jnp.logical_not(edge))
        def _():
            for k in range(3):
                ext[k, at:at + 32, :] = jnp.zeros((32, LANES), jnp.float32)

    @pl.when(owner)
    def _():
        for src, i in ((send1, 0), (send2, 2)):
            part = src.at[:, pl.ds(0, src.shape[1] - 2)]
            pltpu.make_async_copy(part, part, sems.at[i]).wait()

    @pl.when(jnp.logical_not(owner))
    def _():
        pltpu.make_async_copy(send1, send1, sems.at[0]).wait()

    for dd in (-1, 1):
        near(dd, 0).wait()
    for there, to in ((north, -1), (south, 1)):
        @pl.when(there)
        def _():
            for dd in (-1, 0, 1):
                near(dd, to).wait_send()
                near(dd, -to).wait_recv()


def memo(f):
    seen = {}

    def g(i):
        if i not in seen:
            seen[i] = f(i)
        return seen[i]

    return g


def v_cycle(load, c0, inside):
    lane = lane_iota(8)

    def coefs(c):
        diag = 1.0 + 4.0 * c
        beta = inside * (0.8 / diag)
        return diag, c * inside, beta, beta * c

    diag0, mult0, beta0, gamma0 = coefs(c0)
    diag1, mult1, beta1, gamma1 = coefs(c0 * 0.25)
    diag2, mult2, beta2, gamma2 = coefs(c0 * 0.0625)

    def pairs(x, step):
        def f(i):
            return (x(i - 1) + x(i + 1)) + (roll(x(i), step) + roll(x(i), -step))
        return f

    def second(first, gamma, step):
        s = pairs(first, step)
        return memo(lambda i: 1.2 * first(i) + gamma * s(i))

    def sweep(x, first, gamma, step):
        s = pairs(x, step)
        return memo(lambda i: (0.2 * x(i) + first(i)) + gamma * s(i))

    def defect(x, rhs, diag, mult, step):
        s = pairs(x, step)
        return memo(lambda i: (rhs(i) - diag * x(i)) + mult * s(i))

    def restrict(x, step):
        even = (lane // step) % 2 == 0

        def f(i):
            q = x(2 * i) + x(2 * i + 1)
            return 0.25 * (q + jnp.where(even, roll(q, -step), roll(q, step)))
        return memo(f)

    dep = memo(load)
    first0 = memo(lambda i: beta0 * dep(i))
    x0 = second(first0, gamma0, 1)
    rhs1 = restrict(defect(x0, dep, diag0, mult0, 1), 1)
    first1 = memo(lambda i: beta1 * rhs1(i))
    x1 = second(first1, gamma1, 2)
    rhs2 = restrict(defect(x1, rhs1, diag1, mult1, 2), 2)
    first2 = memo(lambda i: beta2 * rhs2(i))
    x2 = second(first2, gamma2, 4)
    x2 = sweep(x2, first2, gamma2, 4)
    x2 = sweep(x2, first2, gamma2, 4)
    y1 = memo(lambda i: x1(i) + x2(i >> 1))
    y1 = sweep(y1, first1, gamma1, 2)
    y1 = sweep(y1, first1, gamma1, 2)
    y0 = memo(lambda i: x0(i) + y1(i >> 1))
    y0 = sweep(y0, first0, gamma0, 1)
    return sweep(y0, first0, gamma0, 1)


def window(rows):
    lane = lane_iota(8)

    def load(i):
        k, hi, r = (i + 32) // 32, (i % 32) // 16, i % 16
        before, here, after = rows(k, r), rows(k, r + 32), rows(k, r + 64)
        if hi == 0:
            sides = roll(jnp.where(lane < 32, after, before), -32)
            return jnp.where((lane >= 32) & (lane < 96), roll(here, 32), sides)
        sides = roll(jnp.where(lane < 96, after, before), 32)
        return jnp.where((lane >= 32) & (lane < 96), roll(here, -32), sides)

    return load


def inside_of(g):
    chunk, lane = sub_iota() // 2, lane_iota(8)
    out = ((g == 0) & (chunk == 0) & (lane < 32)) | ((g == NLATDEV - 1) & (chunk == 3) & (lane >= 96))
    return jnp.where(out, 0.0, 1.0)


def cycle_kernel(ext, helm, out, rows):
    g = lax.axis_index("lat")
    lev = sub_iota() % 2
    c0 = jnp.where(lev == 0, jnp.full((8, LANES), helm[0], jnp.float32), jnp.full((8, LANES), helm[1], jnp.float32))
    result = v_cycle(window(lambda k, at: ext[k, pl.ds(at, 8, stride=16), :]), c0, inside_of(g))
    for i in range(32):
        rows[8 * i:8 * i + 8, :] = result(i)
    low = lane_iota(8) < 64
    for block in range(4):
        for lev in range(2):
            for pair in range(2):
                left = rows[pl.ds(64 * block + 4 * pair + lev, 8, stride=8), :]
                right = rows[pl.ds(64 * block + 4 * pair + 2 + lev, 8, stride=8), :]
                out[lev, 8 * block:8 * block + 8, 128 * pair:128 * pair + 128] = jnp.where(
                    low, roll(left, -32), roll(right, 32))


def per_device(field, offsets, fraction, helm):
    vmem = pl.BlockSpec(memory_space=pltpu.VMEM)
    smem = pl.BlockSpec(memory_space=pltpu.SMEM)
    hbm = pl.BlockSpec(memory_space=pltpu.HBM)
    parts = pltpu.VMEM((REP, 2 * OWNERS, LANES), jnp.float32)
    circles = pltpu.VMEM((REP, LANES, LANES), jnp.float32)
    ext = pl.pallas_call(
        exchange_kernel,
        out_shape=jax.ShapeDtypeStruct((3, 192, LANES), jnp.float32),
        in_specs=[hbm, hbm, hbm],
        out_specs=vmem,
        scratch_shapes=[
            pltpu.VMEM(field.shape, jnp.float32),
            pltpu.SMEM(offsets.shape, jnp.int32),
            pltpu.SMEM(fraction.shape, jnp.float32),
            parts, circles, circles, parts, circles,
            pltpu.SemaphoreType.DMA((3,)),
            pltpu.SemaphoreType.DMA((4,)),
            pltpu.SemaphoreType.DMA((3, 3)),
            pltpu.SemaphoreType.DMA((3, 3)),
        ],
        compiler_params=pltpu.CompilerParams(collective_id=0, has_side_effects=True, vmem_limit_bytes=16 * 1024 * 1024),
    )(field, offsets, fraction)
    return pl.pallas_call(
        cycle_kernel,
        out_shape=jax.ShapeDtypeStruct(field.shape, jnp.float32),
        in_specs=[vmem, smem],
        out_specs=vmem,
        scratch_shapes=[pltpu.VMEM((256, LANES), jnp.float32)],
        compiler_params=pltpu.CompilerParams(vmem_limit_bytes=16 * 1024 * 1024),
    )(ext, helm)


def solution(mesh):
    return jax.shard_map(
        per_device,
        mesh=mesh,
        in_specs=(P(None, "lon", "lat"), P("lat"), P("lat"), P()),
        out_specs=P(None, "lon", "lat"),
        check_vma=False,
    )
```

```python
import jax
import jax.numpy as jnp
from jax import lax
from jax.experimental import pallas as pl
from jax.experimental.pallas import tpu as pltpu
from jax.sharding import PartitionSpec as P

MESH = pl.DeviceIdType.MESH
NLONDEV = 64
NLATDEV = 8
OWNERS = 32
REP = NLONDEV // OWNERS
LANES = 128


def roll(x, shift):
    return pltpu.roll(x, shift % LANES, 1)


def lane_iota(rows):
    return lax.broadcasted_iota(jnp.int32, (rows, LANES), 1)


def sub_iota():
    return lax.broadcasted_iota(jnp.int32, (8, LANES), 0)


def pack_field(half):
    low = lane_iota(16) < 64
    pieces = []
    for chunk in range(4):
        for lev in range(2):
            first, second = half(lev, 0, chunk // 2), half(lev, 1, chunk // 2)
            if chunk % 2 == 0:
                pieces.append(jnp.where(low, first, roll(second, 64)))
            else:
                pieces.append(jnp.where(low, roll(first, 64), second))
    return jnp.concatenate(pieces, axis=0)


def by_chunk(values, dtype):
    chunk = sub_iota() // 2
    full = jnp.full((8, LANES), values[0], dtype)
    for c in range(1, 4):
        full = jnp.where(chunk == c, jnp.full((8, LANES), values[c], dtype), full)
    return full


def shift_rows(v, offset):
    coarse, fine = offset // 16, offset % 16
    for bit in range(7):
        take = (coarse // (1 << bit)) % 2 == 1
        v = [jnp.where(take, roll(x, 1 << bit), x) for x in v]
    for bit in range(4):
        by = 1 << bit
        take = (fine // by) % 2 == 1
        v = [jnp.where(take, v[r - by] if r >= by else roll(v[r - by + 16], 1), v[r]) for r in range(16)]
    return v


def interpolate(g, s):
    w_one = -s * (s - 1.0) * (s - 2.0) / 6.0
    w_two = (s + 1.0) * (s - 1.0) * (s - 2.0) / 2.0
    w_three = -(s + 1.0) * s * (s - 2.0) / 2.0
    w_four = (s + 1.0) * s * (s - 1.0) / 6.0
    ext = [roll(g[14], 1), roll(g[15], 1)] + g + [roll(g[0], -1)]
    return [w_one * ext[r + 3] + w_two * ext[r + 2] + w_three * ext[r + 1] + w_four * ext[r] for r in range(16)]


def exchange_kernel(field_in, offsets_in, fraction_in, ext, field, offsets, fraction, send1, recv1, send2, recv2, work,
                    load_sems, sems, near_send, near_recv):
    d = lax.axis_index("lon")
    g = lax.axis_index("lat")
    north, south = g > 0, g < NLATDEV - 1
    owner = d < OWNERS

    loads = [pltpu.make_async_copy(src, dst, load_sems.at[i]) for i, (src, dst) in enumerate(
        ((field_in, field), (offsets_in, offsets), (fraction_in, fraction)))]
    for load in loads:
        load.start()

    barrier = pltpu.get_barrier_semaphore()

    for there, to in ((north, -1), (south, 1)):
        @pl.when(there)
        def _():
            for dd in (-1, 0, 1):
                pl.semaphore_signal(
                    barrier, inc=1,
                    device_id={"lon": lax.rem(d + dd + NLONDEV, NLONDEV), "lat": g + to},
                    device_id_type=MESH)

    @pl.when(owner)
    def _():
        def greet(j, carry):
            pl.semaphore_signal(barrier, inc=1, device_id={"lon": lax.rem(d + j, NLONDEV)}, device_id_type=MESH)
            return carry

        lax.fori_loop(1, NLONDEV, greet, 0)

    loads[0].wait()
    packed = pack_field(lambda lev, hi, pair: field[lev, 16 * hi:16 * hi + 16, 128 * pair:128 * pair + 128]).T
    for hi in range(2):
        for s in range(REP):
            at = 64 * hi + OWNERS * s
            send1[s, pl.ds(hi, OWNERS, stride=2), :] = packed[at:at + OWNERS]

    one = owner.astype(jnp.int32)
    pl.semaphore_wait(barrier, OWNERS - one + 3 * (north.astype(jnp.int32) + south.astype(jnp.int32)))
    mine = pl.ds(2 * d, 2)

    def collect(j, carry):
        to = lax.rem(d + j, OWNERS)
        pltpu.make_async_remote_copy(
            src_ref=send1.at[:, pl.ds(2 * to, 2)], dst_ref=recv1.at[:, mine],
            send_sem=sems.at[0], recv_sem=sems.at[1],
            device_id={"lon": to}, device_id_type=MESH,
        ).start()
        return carry

    lax.fori_loop(one, OWNERS, collect, 0)
    loads[1].wait()
    loads[2].wait()

    @pl.when(owner)
    def _():
        pltpu.make_async_copy(send1.at[:, mine], recv1.at[:, mine], sems.at[1]).start()
        pltpu.make_async_copy(recv1, recv1, sems.at[1]).wait()
        for s in range(REP):
            work[s] = recv1[s].T
            v = [work[s, pl.ds(r, 8, stride=16), :] for r in range(16)]
            own = [d + OWNERS * s + 64 * c for c in range(4)]
            v = shift_rows(v, by_chunk([offsets[i] for i in own], jnp.int32))
            v = interpolate(v, by_chunk([fraction[i] for i in own], jnp.float32))
            for r in range(16):
                work[s, pl.ds(r, 8, stride=16), :] = v[r]
            send2[s] = work[s].T

        def spread(j, carry):
            to = j - lax.rem(j, 4) + lax.rem(j + d, 4)

            @pl.when(to != d)
            def _():
                pltpu.make_async_remote_copy(
                    src_ref=send2.at[:, pl.ds(2 * to, 2)], dst_ref=recv2.at[:, mine],
                    send_sem=sems.at[2], recv_sem=sems.at[3],
                    device_id={"lon": to}, device_id_type=MESH,
                ).start()
            return carry

        lax.fori_loop(0, NLONDEV, spread, 0)
        pltpu.make_async_copy(send2.at[:, mine], recv2.at[:, mine], sems.at[3]).start()

    pltpu.make_async_copy(recv2, recv2, sems.at[3]).wait()
    ext[1, 32:160, :] = jnp.concatenate(
        [recv2[s, pl.ds(hi, OWNERS, stride=2), :] for hi in range(2) for s in range(REP)], axis=0).T

    def near(dd, to):
        if to == 0:
            src, dst = ext.at[1, pl.ds(32, 128)], ext.at[1 - dd, pl.ds(32, 128)]
        elif to < 0:
            src, dst = ext.at[1, pl.ds(32, 32)], ext.at[1 - dd, pl.ds(160, 32)]
        else:
            src, dst = ext.at[1, pl.ds(128, 32)], ext.at[1 - dd, pl.ds(0, 32)]
        return pltpu.make_async_remote_copy(
            src_ref=src, dst_ref=dst,
            send_sem=near_send.at[to + 1, dd + 1], recv_sem=near_recv.at[to + 1, dd + 1],
            device_id={"lon": lax.rem(d + dd + NLONDEV, NLONDEV), "lat": g + to},
            device_id_type=MESH)

    for dd in (-1, 1):
        near(dd, 0).start()
    for there, to in ((north, -1), (south, 1)):
        @pl.when(there)
        def _():
            for dd in (-1, 0, 1):
                near(dd, to).start()
    for edge, at in ((north, 0), (south, 160)):
        @pl.when(jnp.logical_not(edge))
        def _():
            for k in range(3):
                ext[k, at:at + 32, :] = jnp.zeros((32, LANES), jnp.float32)

    @pl.when(owner)
    def _():
        for src, i in ((send1, 0), (send2, 2)):
            part = src.at[:, pl.ds(0, src.shape[1] - 2)]
            pltpu.make_async_copy(part, part, sems.at[i]).wait()

    @pl.when(jnp.logical_not(owner))
    def _():
        pltpu.make_async_copy(send1, send1, sems.at[0]).wait()

    for dd in (-1, 1):
        near(dd, 0).wait()
    for there, to in ((north, -1), (south, 1)):
        @pl.when(there)
        def _():
            for dd in (-1, 0, 1):
                near(dd, to).wait_send()
                near(dd, -to).wait_recv()


def memo(f):
    seen = {}

    def g(i):
        if i not in seen:
            seen[i] = f(i)
        return seen[i]

    return g


def v_cycle(load, c0, inside):
    lane = lane_iota(8)

    def coefs(c):
        diag = 1.0 + 4.0 * c
        beta = inside * (0.8 / diag)
        return diag, c * inside, beta, beta * c

    diag0, mult0, beta0, gamma0 = coefs(c0)
    diag1, mult1, beta1, gamma1 = coefs(c0 * 0.25)
    diag2, mult2, beta2, gamma2 = coefs(c0 * 0.0625)

    def pairs(x, step):
        def f(i):
            return (x(i - 1) + x(i + 1)) + (roll(x(i), step) + roll(x(i), -step))
        return f

    def second(first, gamma, step):
        s = pairs(first, step)
        return memo(lambda i: 1.2 * first(i) + gamma * s(i))

    def sweep(x, first, gamma, step):
        s = pairs(x, step)
        return memo(lambda i: (0.2 * x(i) + first(i)) + gamma * s(i))

    def defect(x, rhs, diag, mult, step):
        s = pairs(x, step)
        return memo(lambda i: (rhs(i) - diag * x(i)) + mult * s(i))

    def restrict(x, step):
        even = (lane // step) % 2 == 0

        def f(i):
            q = x(2 * i) + x(2 * i + 1)
            return 0.25 * (q + jnp.where(even, roll(q, -step), roll(q, step)))
        return memo(f)

    dep = memo(load)
    first0 = memo(lambda i: beta0 * dep(i))
    x0 = second(first0, gamma0, 1)
    rhs1 = restrict(defect(x0, dep, diag0, mult0, 1), 1)
    first1 = memo(lambda i: beta1 * rhs1(i))
    x1 = second(first1, gamma1, 2)
    rhs2 = restrict(defect(x1, rhs1, diag1, mult1, 2), 2)
    first2 = memo(lambda i: beta2 * rhs2(i))
    x2 = second(first2, gamma2, 4)
    x2 = sweep(x2, first2, gamma2, 4)
    x2 = sweep(x2, first2, gamma2, 4)
    y1 = memo(lambda i: x1(i) + x2(i >> 1))
    y1 = sweep(y1, first1, gamma1, 2)
    y1 = sweep(y1, first1, gamma1, 2)
    y0 = memo(lambda i: x0(i) + y1(i >> 1))
    y0 = sweep(y0, first0, gamma0, 1)
    return sweep(y0, first0, gamma0, 1)


def window(rows):
    lane = lane_iota(8)

    def load(i):
        k, hi, r = (i + 32) // 32, (i % 32) // 16, i % 16
        before, here, after = rows(k, r), rows(k, r + 32), rows(k, r + 64)
        if hi == 0:
            sides = roll(jnp.where(lane < 32, after, before), -32)
            return jnp.where((lane >= 32) & (lane < 96), roll(here, 32), sides)
        sides = roll(jnp.where(lane < 96, after, before), 32)
        return jnp.where((lane >= 32) & (lane < 96), roll(here, -32), sides)

    return load


def inside_of(g):
    chunk, lane = sub_iota() // 2, lane_iota(8)
    out = ((g == 0) & (chunk == 0) & (lane < 32)) | ((g == NLATDEV - 1) & (chunk == 3) & (lane >= 96))
    return jnp.where(out, 0.0, 1.0)


def cycle_kernel(ext, helm, out, rows):
    g = lax.axis_index("lat")
    lev = sub_iota() % 2
    c0 = jnp.where(lev == 0, jnp.full((8, LANES), helm[0], jnp.float32), jnp.full((8, LANES), helm[1], jnp.float32))
    result = v_cycle(window(lambda k, at: ext[k, pl.ds(at, 8, stride=16), :]), c0, inside_of(g))
    for i in range(32):
        rows[8 * i:8 * i + 8, :] = result(i)
    low = lane_iota(8) < 64
    for block in range(4):
        for lev in range(2):
            for pair in range(2):
                left = rows[pl.ds(64 * block + 4 * pair + lev, 8, stride=8), :]
                right = rows[pl.ds(64 * block + 4 * pair + 2 + lev, 8, stride=8), :]
                out[lev, 8 * block:8 * block + 8, 128 * pair:128 * pair + 128] = jnp.where(
                    low, roll(left, -32), roll(right, 32))


def per_device(field, offsets, fraction, helm):
    vmem = pl.BlockSpec(memory_space=pltpu.VMEM)
    smem = pl.BlockSpec(memory_space=pltpu.SMEM)
    hbm = pl.BlockSpec(memory_space=pltpu.HBM)
    parts = pltpu.VMEM((REP, 2 * OWNERS, LANES), jnp.float32)
    circles = pltpu.VMEM((REP, LANES, LANES), jnp.float32)
    ext = pl.pallas_call(
        exchange_kernel,
        out_shape=jax.ShapeDtypeStruct((3, 192, LANES), jnp.float32),
        in_specs=[hbm, hbm, hbm],
        out_specs=vmem,
        scratch_shapes=[
            pltpu.VMEM(field.shape, jnp.float32),
            pltpu.SMEM(offsets.shape, jnp.int32),
            pltpu.SMEM(fraction.shape, jnp.float32),
            parts, circles, circles, parts, circles,
            pltpu.SemaphoreType.DMA((3,)),
            pltpu.SemaphoreType.DMA((4,)),
            pltpu.SemaphoreType.DMA((3, 3)),
            pltpu.SemaphoreType.DMA((3, 3)),
        ],
        compiler_params=pltpu.CompilerParams(collective_id=0, has_side_effects=True, vmem_limit_bytes=16 * 1024 * 1024),
    )(*(pltpu.with_memory_space_constraint(a, pltpu.HBM) for a in (field, offsets, fraction)))
    return pl.pallas_call(
        cycle_kernel,
        out_shape=jax.ShapeDtypeStruct(field.shape, jnp.float32),
        in_specs=[vmem, smem],
        out_specs=vmem,
        scratch_shapes=[pltpu.VMEM((256, LANES), jnp.float32)],
        compiler_params=pltpu.CompilerParams(vmem_limit_bytes=16 * 1024 * 1024),
    )(ext, helm)


def solution(mesh):
    return jax.shard_map(
        per_device,
        mesh=mesh,
        in_specs=(P(None, "lon", "lat"), P("lat"), P("lat"), P()),
        out_specs=P(None, "lon", "lat"),
        check_vma=False,
    )
```

```python
import jax
import jax.numpy as jnp
from jax import lax
from jax.experimental import pallas as pl
from jax.experimental.pallas import tpu as pltpu
from jax.sharding import PartitionSpec as P

MESH = pl.DeviceIdType.MESH
NLONDEV = 64
NLATDEV = 8
FIRST = 0
PLANES = 4
OWNERS = 4 * PLANES
REP = NLONDEV // OWNERS
LANES = 128


def roll(x, shift):
    return pltpu.roll(x, shift % LANES, 1)


def lane_iota(rows):
    return lax.broadcasted_iota(jnp.int32, (rows, LANES), 1)


def sub_iota():
    return lax.broadcasted_iota(jnp.int32, (8, LANES), 0)


def pack_field(half):
    low = lane_iota(16) < 64
    pieces = []
    for chunk in range(4):
        for lev in range(2):
            first, second = half(lev, 0, chunk // 2), half(lev, 1, chunk // 2)
            if chunk % 2 == 0:
                pieces.append(jnp.where(low, first, roll(second, 64)))
            else:
                pieces.append(jnp.where(low, roll(first, 64), second))
    return jnp.concatenate(pieces, axis=0)


def by_chunk(values, dtype):
    chunk = sub_iota() // 2
    full = jnp.full((8, LANES), values[0], dtype)
    for c in range(1, 4):
        full = jnp.where(chunk == c, jnp.full((8, LANES), values[c], dtype), full)
    return full


def shift_rows(v, offset):
    coarse, fine = offset // 16, offset % 16
    for bit in range(7):
        take = (coarse // (1 << bit)) % 2 == 1
        v = [jnp.where(take, roll(x, 1 << bit), x) for x in v]
    for bit in range(4):
        by = 1 << bit
        take = (fine // by) % 2 == 1
        v = [jnp.where(take, v[r - by] if r >= by else roll(v[r - by + 16], 1), v[r]) for r in range(16)]
    return v


def interpolate(g, s):
    w_one = -s * (s - 1.0) * (s - 2.0) / 6.0
    w_two = (s + 1.0) * (s - 1.0) * (s - 2.0) / 2.0
    w_three = -(s + 1.0) * s * (s - 2.0) / 2.0
    w_four = (s + 1.0) * s * (s - 1.0) / 6.0
    ext = [roll(g[14], 1), roll(g[15], 1)] + g + [roll(g[0], -1)]
    return [w_one * ext[r + 3] + w_two * ext[r + 2] + w_three * ext[r + 1] + w_four * ext[r] for r in range(16)]


def exchange_kernel(field_in, offsets_in, fraction_in, ext, field, offsets, fraction, send1, recv1, send2, recv2, work,
                    load_sems, sems, near_send, near_recv):
    d = lax.axis_index("lon")
    g = lax.axis_index("lat")
    north, south = g > 0, g < NLATDEV - 1
    rank = lax.rem(d + NLONDEV - 4 * FIRST, NLONDEV)
    owner = rank < OWNERS

    loads = [pltpu.make_async_copy(src, dst, load_sems.at[i]) for i, (src, dst) in enumerate(
        ((field_in, field), (offsets_in, offsets), (fraction_in, fraction)))]
    for load in loads:
        load.start()

    barrier = pltpu.get_barrier_semaphore()

    for there, to in ((north, -1), (south, 1)):
        @pl.when(there)
        def _():
            for dd in (-1, 0, 1):
                pl.semaphore_signal(
                    barrier, inc=1,
                    device_id={"lon": lax.rem(d + dd + NLONDEV, NLONDEV), "lat": g + to},
                    device_id_type=MESH)

    @pl.when(owner)
    def _():
        def greet(j, carry):
            pl.semaphore_signal(barrier, inc=1, device_id={"lon": lax.rem(d + j, NLONDEV)}, device_id_type=MESH)
            return carry

        lax.fori_loop(1, NLONDEV, greet, 0)

    loads[0].wait()
    packed = pack_field(lambda lev, hi, pair: field[lev, 16 * hi:16 * hi + 16, 128 * pair:128 * pair + 128]).T
    for hi in range(2):
        for s in range(REP):
            at = 64 * hi + OWNERS * s
            send1[s, pl.ds(hi, OWNERS, stride=2), :] = packed[at:at + OWNERS]

    one = owner.astype(jnp.int32)
    pl.semaphore_wait(barrier, OWNERS - one + 3 * (north.astype(jnp.int32) + south.astype(jnp.int32)))
    mine, ranked = pl.ds(2 * d, 2), pl.ds(2 * rank, 2)

    def collect(j, carry):
        to_rank = lax.rem(rank + j, OWNERS)
        to = lax.rem(to_rank + 4 * FIRST, NLONDEV)
        pltpu.make_async_remote_copy(
            src_ref=send1.at[:, pl.ds(2 * to_rank, 2)], dst_ref=recv1.at[:, mine],
            send_sem=sems.at[0], recv_sem=sems.at[1],
            device_id={"lon": to}, device_id_type=MESH,
        ).start()
        return carry

    lax.fori_loop(one, OWNERS, collect, 0)
    loads[1].wait()
    loads[2].wait()

    @pl.when(owner)
    def _():
        pltpu.make_async_copy(send1.at[:, ranked], recv1.at[:, mine], sems.at[1]).start()
        pltpu.make_async_copy(recv1, recv1, sems.at[1]).wait()
        for s in range(REP):
            work[s] = recv1[s].T
            v = [work[s, pl.ds(r, 8, stride=16), :] for r in range(16)]
            own = [rank + OWNERS * s + 64 * c for c in range(4)]
            v = shift_rows(v, by_chunk([offsets[i] for i in own], jnp.int32))
            v = interpolate(v, by_chunk([fraction[i] for i in own], jnp.float32))
            for r in range(16):
                work[s, pl.ds(r, 8, stride=16), :] = v[r]
            send2[s] = work[s].T

        def spread(j, carry):
            k = j // 4 - PLANES
            plane = jnp.where(k < 0, k + PLANES, jnp.where(k % 2 == 0, 15 - k // 2, PLANES + k // 2))
            to = lax.rem(4 * (plane + FIRST) + lax.rem(j + d, 4), NLONDEV)

            @pl.when(to != d)
            def _():
                pltpu.make_async_remote_copy(
                    src_ref=send2.at[:, pl.ds(2 * to, 2)], dst_ref=recv2.at[:, ranked],
                    send_sem=sems.at[2], recv_sem=sems.at[3],
                    device_id={"lon": to}, device_id_type=MESH,
                ).start()
            return carry

        lax.fori_loop(0, NLONDEV, spread, 0)
        pltpu.make_async_copy(send2.at[:, mine], recv2.at[:, ranked], sems.at[3]).start()

    pltpu.make_async_copy(recv2, recv2, sems.at[3]).wait()
    ext[1, 32:160, :] = jnp.concatenate(
        [recv2[s, pl.ds(hi, OWNERS, stride=2), :] for hi in range(2) for s in range(REP)], axis=0).T

    def near(dd, to):
        if to == 0:
            src, dst = ext.at[1, pl.ds(32, 128)], ext.at[1 - dd, pl.ds(32, 128)]
        elif to < 0:
            src, dst = ext.at[1, pl.ds(32, 32)], ext.at[1 - dd, pl.ds(160, 32)]
        else:
            src, dst = ext.at[1, pl.ds(128, 32)], ext.at[1 - dd, pl.ds(0, 32)]
        return pltpu.make_async_remote_copy(
            src_ref=src, dst_ref=dst,
            send_sem=near_send.at[to + 1, dd + 1], recv_sem=near_recv.at[to + 1, dd + 1],
            device_id={"lon": lax.rem(d + dd + NLONDEV, NLONDEV), "lat": g + to},
            device_id_type=MESH)

    for dd in (-1, 1):
        near(dd, 0).start()
    for there, to in ((north, -1), (south, 1)):
        @pl.when(there)
        def _():
            for dd in (-1, 0, 1):
                near(dd, to).start()
    for edge, at in ((north, 0), (south, 160)):
        @pl.when(jnp.logical_not(edge))
        def _():
            for k in range(3):
                ext[k, at:at + 32, :] = jnp.zeros((32, LANES), jnp.float32)

    @pl.when(owner)
    def _():
        for src, i in ((send1, 0), (send2, 2)):
            part = src.at[:, pl.ds(0, src.shape[1] - 2)]
            pltpu.make_async_copy(part, part, sems.at[i]).wait()

    @pl.when(jnp.logical_not(owner))
    def _():
        pltpu.make_async_copy(send1, send1, sems.at[0]).wait()

    for dd in (-1, 1):
        near(dd, 0).wait()
    for there, to in ((north, -1), (south, 1)):
        @pl.when(there)
        def _():
            for dd in (-1, 0, 1):
                near(dd, to).wait_send()
                near(dd, -to).wait_recv()


def memo(f):
    seen = {}

    def g(i):
        if i not in seen:
            seen[i] = f(i)
        return seen[i]

    return g


def v_cycle(load, c0, inside):
    lane = lane_iota(8)

    def coefs(c):
        diag = 1.0 + 4.0 * c
        beta = inside * (0.8 / diag)
        return diag, c * inside, beta, beta * c

    diag0, mult0, beta0, gamma0 = coefs(c0)
    diag1, mult1, beta1, gamma1 = coefs(c0 * 0.25)
    diag2, mult2, beta2, gamma2 = coefs(c0 * 0.0625)

    def pairs(x, step):
        def f(i):
            return (x(i - 1) + x(i + 1)) + (roll(x(i), step) + roll(x(i), -step))
        return f

    def second(first, gamma, step):
        s = pairs(first, step)
        return memo(lambda i: 1.2 * first(i) + gamma * s(i))

    def sweep(x, first, gamma, step):
        s = pairs(x, step)
        return memo(lambda i: (0.2 * x(i) + first(i)) + gamma * s(i))

    def defect(x, rhs, diag, mult, step):
        s = pairs(x, step)
        return memo(lambda i: (rhs(i) - diag * x(i)) + mult * s(i))

    def restrict(x, step):
        even = (lane // step) % 2 == 0

        def f(i):
            q = x(2 * i) + x(2 * i + 1)
            return 0.25 * (q + jnp.where(even, roll(q, -step), roll(q, step)))
        return memo(f)

    def all_of(f, low, high):
        for i in range(low, high + 1):
            f(i)
        return f

    dep = all_of(memo(load), -26, 57)
    first0 = all_of(memo(lambda i: beta0 * dep(i)), -26, 57)
    x0 = all_of(second(first0, gamma0, 1), -25, 56)
    rhs1 = all_of(restrict(all_of(defect(x0, dep, diag0, mult0, 1), -24, 55), 1), -12, 27)
    first1 = all_of(memo(lambda i: beta1 * rhs1(i)), -12, 27)
    x1 = all_of(second(first1, gamma1, 2), -11, 26)
    rhs2 = all_of(restrict(all_of(defect(x1, rhs1, diag1, mult1, 2), -10, 25), 2), -5, 12)
    first2 = all_of(memo(lambda i: beta2 * rhs2(i)), -5, 12)
    x2 = all_of(second(first2, gamma2, 4), -4, 11)
    x2 = all_of(sweep(x2, first2, gamma2, 4), -3, 10)
    x2 = all_of(sweep(x2, first2, gamma2, 4), -2, 9)
    y1 = all_of(memo(lambda i: x1(i) + x2(i >> 1)), -3, 18)
    y1 = all_of(sweep(y1, first1, gamma1, 2), -2, 17)
    y1 = all_of(sweep(y1, first1, gamma1, 2), -1, 16)
    y0 = all_of(memo(lambda i: x0(i) + y1(i >> 1)), -2, 33)
    y0 = all_of(sweep(y0, first0, gamma0, 1), -1, 32)
    return sweep(y0, first0, gamma0, 1)


def window(rows):
    lane = lane_iota(8)

    def load(i):
        k, hi, r = (i + 32) // 32, (i % 32) // 16, i % 16
        before, here, after = rows(k, r), rows(k, r + 32), rows(k, r + 64)
        if hi == 0:
            sides = roll(jnp.where(lane < 32, after, before), -32)
            return jnp.where((lane >= 32) & (lane < 96), roll(here, 32), sides)
        sides = roll(jnp.where(lane < 96, after, before), 32)
        return jnp.where((lane >= 32) & (lane < 96), roll(here, -32), sides)

    return load


def inside_of(g):
    chunk, lane = sub_iota() // 2, lane_iota(8)
    out = ((g == 0) & (chunk == 0) & (lane < 32)) | ((g == NLATDEV - 1) & (chunk == 3) & (lane >= 96))
    return jnp.where(out, 0.0, 1.0)


def cycle_kernel(ext, helm, out, rows):
    g = lax.axis_index("lat")
    lev = sub_iota() % 2
    c0 = jnp.where(lev == 0, jnp.full((8, LANES), helm[0], jnp.float32), jnp.full((8, LANES), helm[1], jnp.float32))
    result = v_cycle(window(lambda k, at: ext[k, pl.ds(at, 8, stride=16), :]), c0, inside_of(g))
    for i in range(32):
        rows[8 * i:8 * i + 8, :] = result(i)
    low = lane_iota(8) < 64
    for block in range(4):
        for lev in range(2):
            for pair in range(2):
                left = rows[pl.ds(64 * block + 4 * pair + lev, 8, stride=8), :]
                right = rows[pl.ds(64 * block + 4 * pair + 2 + lev, 8, stride=8), :]
                out[lev, 8 * block:8 * block + 8, 128 * pair:128 * pair + 128] = jnp.where(
                    low, roll(left, -32), roll(right, 32))


def per_device(field, offsets, fraction, helm):
    vmem = pl.BlockSpec(memory_space=pltpu.VMEM)
    smem = pl.BlockSpec(memory_space=pltpu.SMEM)
    hbm = pl.BlockSpec(memory_space=pltpu.HBM)
    parts = pltpu.VMEM((REP, 2 * OWNERS, LANES), jnp.float32)
    circles = pltpu.VMEM((REP, LANES, LANES), jnp.float32)
    ext = pl.pallas_call(
        exchange_kernel,
        out_shape=jax.ShapeDtypeStruct((3, 192, LANES), jnp.float32),
        in_specs=[hbm, hbm, hbm],
        out_specs=vmem,
        scratch_shapes=[
            pltpu.VMEM(field.shape, jnp.float32),
            pltpu.SMEM(offsets.shape, jnp.int32),
            pltpu.SMEM(fraction.shape, jnp.float32),
            parts, circles, circles, parts, circles,
            pltpu.SemaphoreType.DMA((3,)),
            pltpu.SemaphoreType.DMA((4,)),
            pltpu.SemaphoreType.DMA((3, 3)),
            pltpu.SemaphoreType.DMA((3, 3)),
        ],
        compiler_params=pltpu.CompilerParams(collective_id=0, has_side_effects=True, vmem_limit_bytes=16 * 1024 * 1024),
    )(*(pltpu.with_memory_space_constraint(a, pltpu.HBM) for a in (field, offsets, fraction)))
    return pl.pallas_call(
        cycle_kernel,
        out_shape=jax.ShapeDtypeStruct(field.shape, jnp.float32),
        in_specs=[vmem, smem],
        out_specs=vmem,
        scratch_shapes=[pltpu.VMEM((256, LANES), jnp.float32)],
        compiler_params=pltpu.CompilerParams(vmem_limit_bytes=16 * 1024 * 1024),
    )(ext, helm)


def solution(mesh):
    return jax.shard_map(
        per_device,
        mesh=mesh,
        in_specs=(P(None, "lon", "lat"), P("lat"), P("lat"), P()),
        out_specs=P(None, "lon", "lat"),
        check_vma=False,
    )
```

```python
import jax
import jax.numpy as jnp
from jax import lax
from jax.experimental import pallas as pl
from jax.experimental.pallas import tpu as pltpu
from jax.sharding import PartitionSpec as P

MESH = pl.DeviceIdType.MESH
NLONDEV = 64
NLATDEV = 8
FIRST = 0
PLANES = 4
OWNERS = 4 * PLANES
REP = NLONDEV // OWNERS
LANES = 128


def roll(x, shift):
    return pltpu.roll(x, shift % LANES, 1)


def lane_iota(rows):
    return lax.broadcasted_iota(jnp.int32, (rows, LANES), 1)


def sub_iota():
    return lax.broadcasted_iota(jnp.int32, (8, LANES), 0)


def pack_field(half):
    low = lane_iota(16) < 64
    pieces = []
    for chunk in range(4):
        for lev in range(2):
            first, second = half(lev, 0, chunk // 2), half(lev, 1, chunk // 2)
            if chunk % 2 == 0:
                pieces.append(jnp.where(low, first, roll(second, 64)))
            else:
                pieces.append(jnp.where(low, roll(first, 64), second))
    return jnp.concatenate(pieces, axis=0)


def by_chunk(chunk, values, dtype):
    full = jnp.full((8, LANES), values[0], dtype)
    for c in range(1, 4):
        full = jnp.where(chunk == c, jnp.full((8, LANES), values[c], dtype), full)
    return full


def shift_coarse(x, offset):
    v = [x[8 * i:8 * i + 8] for i in range(16)]
    sub = sub_iota()
    for bit in range(7):
        by = 1 << bit
        take = (offset // (16 * by)) % 2 == 1
        if by < 8:
            turned = [pltpu.roll(u, by, 0) for u in v]
            moved = [jnp.where(sub < by, turned[i - 1], turned[i]) for i in range(16)]
        else:
            moved = [v[i - by // 8] for i in range(16)]
        v = [jnp.where(take, m, u) for m, u in zip(moved, v)]
    return jnp.concatenate(v, axis=0)


def shift_fine(v, offset):
    for bit in range(4):
        by = 1 << bit
        take = (offset // by) % 2 == 1
        v = [jnp.where(take, v[r - by] if r >= by else roll(v[r - by + 16], 1), v[r]) for r in range(16)]
    return v


def interpolate(g, s):
    w_one = -s * (s - 1.0) * (s - 2.0) / 6.0
    w_two = (s + 1.0) * (s - 1.0) * (s - 2.0) / 2.0
    w_three = -(s + 1.0) * s * (s - 2.0) / 2.0
    w_four = (s + 1.0) * s * (s - 1.0) / 6.0
    ext = [roll(g[14], 1), roll(g[15], 1)] + g + [roll(g[0], -1)]
    return [w_one * ext[r + 3] + w_two * ext[r + 2] + w_three * ext[r + 1] + w_four * ext[r] for r in range(16)]


def exchange_kernel(field_in, offsets_in, fraction_in, ext, field, offsets, fraction, send1, recv1, send2, recv2, work,
                    load_sems, sems, near_send, near_recv, lat_in, may_near):
    d = lax.axis_index("lon")
    g = lax.axis_index("lat")
    north, south = g > 0, g < NLATDEV - 1
    rank = lax.rem(d + NLONDEV - 4 * FIRST, NLONDEV)
    owner = rank < OWNERS

    loads = [pltpu.make_async_copy(src, dst, load_sems.at[i]) for i, (src, dst) in enumerate(
        ((field_in, field), (offsets_in, offsets), (fraction_in, fraction)))]
    for load in loads:
        load.start()

    barrier = pltpu.get_barrier_semaphore()

    def tell_lat(sem):
        for there, to in ((north, -1), (south, 1)):
            @pl.when(there)
            def _():
                pl.semaphore_signal(sem, inc=1, device_id={"lat": g + to}, device_id_type=MESH)

    @pl.when(owner)
    def _():
        def greet(j, carry):
            pl.semaphore_signal(barrier, inc=1, device_id={"lon": lax.rem(d + j, NLONDEV)}, device_id_type=MESH)
            return carry

        tell_lat(barrier)
        lax.fori_loop(1, NLONDEV, greet, 0)

    loads[0].wait()
    packed = pack_field(lambda lev, hi, pair: field[lev, 16 * hi:16 * hi + 16, 128 * pair:128 * pair + 128]).T
    for hi in range(2):
        for s in range(REP):
            at = 64 * hi + OWNERS * s
            send1[s, pl.ds(hi, OWNERS, stride=2), :] = packed[at:at + OWNERS]

    one = owner.astype(jnp.int32)
    sides = north.astype(jnp.int32) + south.astype(jnp.int32)
    pl.semaphore_wait(barrier, OWNERS - one + one * sides)
    mine, ranked = pl.ds(2 * d, 2), pl.ds(2 * rank, 2)

    def collect(j, carry):
        to_rank = lax.rem(rank + j, OWNERS)
        to = lax.rem(to_rank + 4 * FIRST, NLONDEV)
        pltpu.make_async_remote_copy(
            src_ref=send1.at[:, pl.ds(2 * to_rank, 2)], dst_ref=recv1.at[:, mine],
            send_sem=sems.at[0], recv_sem=sems.at[1],
            device_id={"lon": to}, device_id_type=MESH,
        ).start()
        return carry

    lax.fori_loop(one, OWNERS, collect, 0)
    loads[1].wait()
    loads[2].wait()

    @pl.when(owner)
    def _():
        pltpu.make_async_copy(send1.at[:, ranked], recv1.at[:, mine], sems.at[1]).start()
        pltpu.make_async_copy(recv1, recv1, sems.at[1]).wait()
        tell_lat(lat_in)
        for s in range(REP):
            own = [rank + OWNERS * s + 64 * c for c in range(4)]
            turns = [offsets[i] for i in own]
            work[s] = shift_coarse(recv1[s], by_chunk(lane_iota(8) // 32, turns, jnp.int32)).T
            v = [work[s, pl.ds(r, 8, stride=16), :] for r in range(16)]
            v = shift_fine(v, by_chunk(sub_iota() // 2, turns, jnp.int32))
            v = interpolate(v, by_chunk(sub_iota() // 2, [fraction[i] for i in own], jnp.float32))
            for r in range(16):
                work[s, pl.ds(r, 8, stride=16), :] = v[r]
            send2[s] = work[s].T

        def spread(j, carry):
            k = j // 4 - PLANES
            plane = jnp.where(k < 0, k + PLANES, jnp.where(k % 2 == 0, 15 - k // 2, PLANES + k // 2))
            to = lax.rem(4 * (plane + FIRST) + lax.rem(j + d, 4), NLONDEV)

            @pl.when(to != d)
            def _():
                pltpu.make_async_remote_copy(
                    src_ref=send2.at[:, pl.ds(2 * to, 2)], dst_ref=recv2.at[:, ranked],
                    send_sem=sems.at[2], recv_sem=sems.at[3],
                    device_id={"lon": to}, device_id_type=MESH,
                ).start()
            return carry

        lax.fori_loop(0, NLONDEV, spread, 0)
        pltpu.make_async_copy(send2.at[:, mine], recv2.at[:, ranked], sems.at[3]).start()
        pl.semaphore_wait(lat_in, sides)
        for i in range(OWNERS, NLONDEV, OWNERS):
            pl.semaphore_signal(may_near, inc=1, device_id={"lon": lax.rem(d + i, NLONDEV)}, device_id_type=MESH)

    pltpu.make_async_copy(recv2, recv2, sems.at[3]).wait()
    ext[1, 32:160, :] = jnp.concatenate(
        [recv2[s, pl.ds(hi, OWNERS, stride=2), :] for hi in range(2) for s in range(REP)], axis=0).T

    def near(dd, to):
        if to == 0:
            src, dst = ext.at[1, pl.ds(32, 128)], ext.at[1 - dd, pl.ds(32, 128)]
        elif to < 0:
            src, dst = ext.at[1, pl.ds(32, 32)], ext.at[1 - dd, pl.ds(160, 32)]
        else:
            src, dst = ext.at[1, pl.ds(128, 32)], ext.at[1 - dd, pl.ds(0, 32)]
        return pltpu.make_async_remote_copy(
            src_ref=src, dst_ref=dst,
            send_sem=near_send.at[to + 1, dd + 1], recv_sem=near_recv.at[to + 1, dd + 1],
            device_id={"lon": lax.rem(d + dd + NLONDEV, NLONDEV), "lat": g + to},
            device_id_type=MESH)

    for dd in (-1, 1):
        near(dd, 0).start()

    @pl.when(jnp.logical_not(owner))
    def _():
        pl.semaphore_wait(may_near, 1)

    for there, to in ((north, -1), (south, 1)):
        @pl.when(there)
        def _():
            for dd in (-1, 0, 1):
                near(dd, to).start()
    for edge, at in ((north, 0), (south, 160)):
        @pl.when(jnp.logical_not(edge))
        def _():
            for k in range(3):
                ext[k, at:at + 32, :] = jnp.zeros((32, LANES), jnp.float32)

    @pl.when(owner)
    def _():
        for src, i in ((send1, 0), (send2, 2)):
            part = src.at[:, pl.ds(0, src.shape[1] - 2)]
            pltpu.make_async_copy(part, part, sems.at[i]).wait()

    @pl.when(jnp.logical_not(owner))
    def _():
        pltpu.make_async_copy(send1, send1, sems.at[0]).wait()

    for dd in (-1, 1):
        near(dd, 0).wait()
    for there, to in ((north, -1), (south, 1)):
        @pl.when(there)
        def _():
            for dd in (-1, 0, 1):
                near(dd, to).wait_send()
                near(dd, -to).wait_recv()


def memo(f):
    seen = {}

    def g(i):
        if i not in seen:
            seen[i] = f(i)
        return seen[i]

    return g


def v_cycle(load, c0, inside):
    lane = lane_iota(8)

    def coefs(c):
        diag = 1.0 + 4.0 * c
        beta = inside * (0.8 / diag)
        return diag, c * inside, beta, beta * c

    diag0, mult0, beta0, gamma0 = coefs(c0)
    diag1, mult1, beta1, gamma1 = coefs(c0 * 0.25)
    diag2, mult2, beta2, gamma2 = coefs(c0 * 0.0625)

    def pairs(x, step):
        def f(i):
            return (x(i - 1) + x(i + 1)) + (roll(x(i), step) + roll(x(i), -step))
        return f

    def second(first, gamma, step):
        s = pairs(first, step)
        return memo(lambda i: 1.2 * first(i) + gamma * s(i))

    def sweep(x, first, gamma, step):
        s = pairs(x, step)
        return memo(lambda i: (0.2 * x(i) + first(i)) + gamma * s(i))

    def defect(x, rhs, diag, mult, step):
        s = pairs(x, step)
        return memo(lambda i: (rhs(i) - diag * x(i)) + mult * s(i))

    def restrict(x, step):
        even = (lane // step) % 2 == 0

        def f(i):
            q = x(2 * i) + x(2 * i + 1)
            return 0.25 * (q + jnp.where(even, roll(q, -step), roll(q, step)))
        return memo(f)

    def all_of(f, low, high):
        for i in range(low, high + 1):
            f(i)
        return f

    dep = all_of(memo(load), -26, 57)
    first0 = all_of(memo(lambda i: beta0 * dep(i)), -26, 57)
    x0 = all_of(second(first0, gamma0, 1), -25, 56)
    rhs1 = all_of(restrict(all_of(defect(x0, dep, diag0, mult0, 1), -24, 55), 1), -12, 27)
    first1 = all_of(memo(lambda i: beta1 * rhs1(i)), -12, 27)
    x1 = all_of(second(first1, gamma1, 2), -11, 26)
    rhs2 = all_of(restrict(all_of(defect(x1, rhs1, diag1, mult1, 2), -10, 25), 2), -5, 12)
    first2 = all_of(memo(lambda i: beta2 * rhs2(i)), -5, 12)
    x2 = all_of(second(first2, gamma2, 4), -4, 11)
    x2 = all_of(sweep(x2, first2, gamma2, 4), -3, 10)
    x2 = all_of(sweep(x2, first2, gamma2, 4), -2, 9)
    y1 = all_of(memo(lambda i: x1(i) + x2(i >> 1)), -3, 18)
    y1 = all_of(sweep(y1, first1, gamma1, 2), -2, 17)
    y1 = all_of(sweep(y1, first1, gamma1, 2), -1, 16)
    y0 = all_of(memo(lambda i: x0(i) + y1(i >> 1)), -2, 33)
    y0 = all_of(sweep(y0, first0, gamma0, 1), -1, 32)
    return sweep(y0, first0, gamma0, 1)


def window(rows):
    lane = lane_iota(8)

    def load(i):
        k, hi, r = (i + 32) // 32, (i % 32) // 16, i % 16
        before, here, after = rows(k, r), rows(k, r + 32), rows(k, r + 64)
        if hi == 0:
            sides = roll(jnp.where(lane < 32, after, before), -32)
            return jnp.where((lane >= 32) & (lane < 96), roll(here, 32), sides)
        sides = roll(jnp.where(lane < 96, after, before), 32)
        return jnp.where((lane >= 32) & (lane < 96), roll(here, -32), sides)

    return load


def inside_of(g):
    chunk, lane = sub_iota() // 2, lane_iota(8)
    out = ((g == 0) & (chunk == 0) & (lane < 32)) | ((g == NLATDEV - 1) & (chunk == 3) & (lane >= 96))
    return jnp.where(out, 0.0, 1.0)


def cycle_kernel(ext, helm, out, rows):
    g = lax.axis_index("lat")
    lev = sub_iota() % 2
    c0 = jnp.where(lev == 0, jnp.full((8, LANES), helm[0], jnp.float32), jnp.full((8, LANES), helm[1], jnp.float32))
    result = v_cycle(window(lambda k, at: ext[k, pl.ds(at, 8, stride=16), :]), c0, inside_of(g))
    for i in range(32):
        rows[8 * i:8 * i + 8, :] = result(i)
    low = lane_iota(8) < 64
    for block in range(4):
        for lev in range(2):
            for pair in range(2):
                left = rows[pl.ds(64 * block + 4 * pair + lev, 8, stride=8), :]
                right = rows[pl.ds(64 * block + 4 * pair + 2 + lev, 8, stride=8), :]
                out[lev, 8 * block:8 * block + 8, 128 * pair:128 * pair + 128] = jnp.where(
                    low, roll(left, -32), roll(right, 32))


def per_device(field, offsets, fraction, helm):
    vmem = pl.BlockSpec(memory_space=pltpu.VMEM)
    smem = pl.BlockSpec(memory_space=pltpu.SMEM)
    hbm = pl.BlockSpec(memory_space=pltpu.HBM)
    parts = pltpu.VMEM((REP, 2 * OWNERS, LANES), jnp.float32)
    circles = pltpu.VMEM((REP, LANES, LANES), jnp.float32)
    ext = pl.pallas_call(
        exchange_kernel,
        out_shape=jax.ShapeDtypeStruct((3, 192, LANES), jnp.float32),
        in_specs=[hbm, hbm, hbm],
        out_specs=vmem,
        scratch_shapes=[
            pltpu.VMEM(field.shape, jnp.float32),
            pltpu.SMEM(offsets.shape, jnp.int32),
            pltpu.SMEM(fraction.shape, jnp.float32),
            parts, circles, circles, parts, circles,
            pltpu.SemaphoreType.DMA((3,)),
            pltpu.SemaphoreType.DMA((4,)),
            pltpu.SemaphoreType.DMA((3, 3)),
            pltpu.SemaphoreType.DMA((3, 3)),
            pltpu.SemaphoreType.REGULAR,
            pltpu.SemaphoreType.REGULAR,
        ],
        compiler_params=pltpu.CompilerParams(collective_id=0, has_side_effects=True, vmem_limit_bytes=16 * 1024 * 1024),
    )(*(pltpu.with_memory_space_constraint(a, pltpu.HBM) for a in (field, offsets, fraction)))
    return pl.pallas_call(
        cycle_kernel,
        out_shape=jax.ShapeDtypeStruct(field.shape, jnp.float32),
        in_specs=[vmem, smem],
        out_specs=vmem,
        scratch_shapes=[pltpu.VMEM((256, LANES), jnp.float32)],
        compiler_params=pltpu.CompilerParams(vmem_limit_bytes=16 * 1024 * 1024),
    )(ext, helm)


def solution(mesh):
    return jax.shard_map(
        per_device,
        mesh=mesh,
        in_specs=(P(None, "lon", "lat"), P("lat"), P("lat"), P()),
        out_specs=P(None, "lon", "lat"),
        check_vma=False,
    )
```

```python
import jax
import jax.numpy as jnp
from jax import lax
from jax.experimental import pallas as pl
from jax.experimental.pallas import tpu as pltpu
from jax.sharding import PartitionSpec as P

MESH = pl.DeviceIdType.MESH
NLONDEV = 64
NLATDEV = 8
FIRST = 0
PLANES = 4
OWNERS = 4 * PLANES
REP = NLONDEV // OWNERS
LANES = 128


def roll(x, shift):
    return pltpu.roll(x, shift % LANES, 1)


def lane_iota(rows):
    return lax.broadcasted_iota(jnp.int32, (rows, LANES), 1)


def sub_iota():
    return lax.broadcasted_iota(jnp.int32, (8, LANES), 0)


def pack_field(half):
    low = lane_iota(16) < 64
    pieces = []
    for chunk in range(4):
        for lev in range(2):
            first, second = half(lev, 0, chunk // 2), half(lev, 1, chunk // 2)
            if chunk % 2 == 0:
                pieces.append(jnp.where(low, first, roll(second, 64)))
            else:
                pieces.append(jnp.where(low, roll(first, 64), second))
    return jnp.concatenate(pieces, axis=0)


def by_chunk(chunk, values, dtype):
    full = jnp.full((8, LANES), values[0], dtype)
    for c in range(1, 4):
        full = jnp.where(chunk == c, jnp.full((8, LANES), values[c], dtype), full)
    return full


def shift_coarse(x, offset):
    v = [x[8 * i:8 * i + 8] for i in range(16)]
    sub = sub_iota()
    for bit in range(7):
        by = 1 << bit
        take = (offset // (16 * by)) % 2 == 1
        if by < 8:
            turned = [pltpu.roll(u, by, 0) for u in v]
            moved = [jnp.where(sub < by, turned[i - 1], turned[i]) for i in range(16)]
        else:
            moved = [v[i - by // 8] for i in range(16)]
        v = [jnp.where(take, m, u) for m, u in zip(moved, v)]
    return jnp.concatenate(v, axis=0)


def shift_fine(v, offset):
    for bit in range(4):
        by = 1 << bit
        take = (offset // by) % 2 == 1
        v = [jnp.where(take, v[r - by] if r >= by else roll(v[r - by + 16], 1), v[r]) for r in range(16)]
    return v


def interpolate(g, s):
    w_one = -s * (s - 1.0) * (s - 2.0) / 6.0
    w_two = (s + 1.0) * (s - 1.0) * (s - 2.0) / 2.0
    w_three = -(s + 1.0) * s * (s - 2.0) / 2.0
    w_four = (s + 1.0) * s * (s - 1.0) / 6.0
    ext = [roll(g[14], 1), roll(g[15], 1)] + g + [roll(g[0], -1)]
    return [w_one * ext[r + 3] + w_two * ext[r + 2] + w_three * ext[r + 1] + w_four * ext[r] for r in range(16)]


def exchange_kernel(field_in, offsets_in, fraction_in, ext, field, offsets, fraction, send1, recv1, send2, recv2, work,
                    beside,
                    load_sems, sems, beside_send, beside_recv, near_send, near_recv, lat_in, may_near):
    d = lax.axis_index("lon")
    g = lax.axis_index("lat")
    north, south = g > 0, g < NLATDEV - 1
    rank = lax.rem(d + NLONDEV - 4 * FIRST, NLONDEV)
    owner = rank < OWNERS

    loads = [pltpu.make_async_copy(src, dst, load_sems.at[i]) for i, (src, dst) in enumerate(
        ((field_in, field), (offsets_in, offsets), (fraction_in, fraction)))]
    for load in loads:
        load.start()

    barrier = pltpu.get_barrier_semaphore()

    def tell_lat(sem):
        for there, to in ((north, -1), (south, 1)):
            @pl.when(there)
            def _():
                pl.semaphore_signal(sem, inc=1, device_id={"lat": g + to}, device_id_type=MESH)

    @pl.when(owner)
    def _():
        def greet(j, carry):
            pl.semaphore_signal(barrier, inc=1, device_id={"lon": lax.rem(d + j, NLONDEV)}, device_id_type=MESH)
            return carry

        tell_lat(barrier)
        lax.fori_loop(1, NLONDEV, greet, 0)

    loads[0].wait()
    packed = pack_field(lambda lev, hi, pair: field[lev, 16 * hi:16 * hi + 16, 128 * pair:128 * pair + 128]).T
    for hi in range(2):
        for s in range(REP):
            at = 64 * hi + OWNERS * s
            send1[s, pl.ds(hi, OWNERS, stride=2), :] = packed[at:at + OWNERS]

    one = owner.astype(jnp.int32)
    sides = north.astype(jnp.int32) + south.astype(jnp.int32)
    pl.semaphore_wait(barrier, OWNERS - one + one * sides)
    mine, ranked = pl.ds(2 * d, 2), pl.ds(2 * rank, 2)

    def collect(j, carry):
        to_rank = lax.rem(rank + j, OWNERS)
        to = lax.rem(to_rank + 4 * FIRST, NLONDEV)
        pltpu.make_async_remote_copy(
            src_ref=send1.at[:, pl.ds(2 * to_rank, 2)], dst_ref=recv1.at[:, mine],
            send_sem=sems.at[0], recv_sem=sems.at[1],
            device_id={"lon": to}, device_id_type=MESH,
        ).start()
        return carry

    lax.fori_loop(one, OWNERS, collect, 0)
    loads[1].wait()
    loads[2].wait()

    @pl.when(owner)
    def _():
        pltpu.make_async_copy(send1.at[:, ranked], recv1.at[:, mine], sems.at[1]).start()
        pltpu.make_async_copy(recv1, recv1, sems.at[1]).wait()
        tell_lat(lat_in)
        for s in range(REP):
            own = [rank + OWNERS * s + 64 * c for c in range(4)]
            turns = [offsets[i] for i in own]
            work[s] = shift_coarse(recv1[s], by_chunk(lane_iota(8) // 32, turns, jnp.int32)).T
            v = [work[s, pl.ds(r, 8, stride=16), :] for r in range(16)]
            v = shift_fine(v, by_chunk(sub_iota() // 2, turns, jnp.int32))
            v = interpolate(v, by_chunk(sub_iota() // 2, [fraction[i] for i in own], jnp.float32))
            for r in range(16):
                work[s, pl.ds(r, 8, stride=16), :] = v[r]
            send2[s] = work[s].T

        def spread(j, carry):
            k = j // 4
            far = k - PLANES - 1
            plane = jnp.where(far % 2 == 0, PLANES + far // 2, 10 + far // 2)
            plane = jnp.where(k == 0, 15, jnp.where(far < 0, k - 1, plane))
            to = lax.rem(4 * (plane + FIRST) + lax.rem(j + d, 4), NLONDEV)

            @pl.when(to != d)
            def _():
                pltpu.make_async_remote_copy(
                    src_ref=send2.at[:, pl.ds(2 * to, 2)], dst_ref=recv2.at[:, ranked],
                    send_sem=sems.at[2], recv_sem=sems.at[3 + rank // 4],
                    device_id={"lon": to}, device_id_type=MESH,
                ).start()
            return carry

        lax.fori_loop(0, NLONDEV, spread, 0)
        pltpu.make_async_copy(send2.at[:, mine], recv2.at[:, ranked], sems.at[3 + rank // 4]).start()
        pl.semaphore_wait(lat_in, sides)
        for i in range(OWNERS, NLONDEV, OWNERS):
            pl.semaphore_signal(may_near, inc=1, device_id={"lon": lax.rem(d + i, NLONDEV)}, device_id_type=MESH)

    falling = (rank >= OWNERS) & (rank < 40)
    for k in range(PLANES):
        p = jnp.where(falling, PLANES - 1 - k, k)
        part = recv2.at[:, pl.ds(pl.multiple_of(8 * p, 8), 8)]
        pltpu.make_async_copy(part, part, sems.at[3 + p]).wait()
        for side, dd in ((0, 1), (1, -1)):
            pltpu.make_async_remote_copy(
                src_ref=part, dst_ref=beside.at[side, :, pl.ds(pl.multiple_of(8 * p, 8), 8)],
                send_sem=beside_send.at[side], recv_sem=beside_recv.at[side],
                device_id={"lon": lax.rem(d + dd + NLONDEV, NLONDEV)}, device_id_type=MESH,
            ).start()

    def turned(rows):
        return jnp.concatenate(
            [rows[s, pl.ds(hi, OWNERS, stride=2), :] for hi in range(2) for s in range(REP)], axis=0).T

    ext[1, 32:160, :] = turned(recv2)

    def near(dd, to):
        if to < 0:
            src, dst = ext.at[1, pl.ds(32, 32)], ext.at[1 - dd, pl.ds(160, 32)]
        else:
            src, dst = ext.at[1, pl.ds(128, 32)], ext.at[1 - dd, pl.ds(0, 32)]
        return pltpu.make_async_remote_copy(
            src_ref=src, dst_ref=dst,
            send_sem=near_send.at[(to + 1) // 2, dd + 1], recv_sem=near_recv.at[(to + 1) // 2, dd + 1],
            device_id={"lon": lax.rem(d + dd + NLONDEV, NLONDEV), "lat": g + to},
            device_id_type=MESH)

    @pl.when(jnp.logical_not(owner))
    def _():
        pl.semaphore_wait(may_near, 1)

    for there, to in ((north, -1), (south, 1)):
        @pl.when(there)
        def _():
            for dd in (-1, 0, 1):
                near(dd, to).start()
    for edge, at in ((north, 0), (south, 160)):
        @pl.when(jnp.logical_not(edge))
        def _():
            for k in range(3):
                ext[k, at:at + 32, :] = jnp.zeros((32, LANES), jnp.float32)

    for side in range(2):
        pltpu.make_async_copy(beside.at[side], beside.at[side], beside_recv.at[side]).wait()
        ext[2 * side, 32:160, :] = turned(beside.at[side])
        pltpu.make_async_copy(recv2, recv2, beside_send.at[side]).wait()
    for there, to in ((north, -1), (south, 1)):
        @pl.when(there)
        def _():
            for dd in (-1, 0, 1):
                near(dd, to).wait_send()
                near(dd, -to).wait_recv()

    @pl.when(owner)
    def _():
        for src, i in ((send1, 0), (send2, 2)):
            part = src.at[:, pl.ds(0, src.shape[1] - 2)]
            pltpu.make_async_copy(part, part, sems.at[i]).wait()

    @pl.when(jnp.logical_not(owner))
    def _():
        pltpu.make_async_copy(send1, send1, sems.at[0]).wait()


def memo(f):
    seen = {}

    def g(i):
        if i not in seen:
            seen[i] = f(i)
        return seen[i]

    return g


def v_cycle(load, c0, inside):
    lane = lane_iota(8)

    def coefs(c):
        diag = 1.0 + 4.0 * c
        beta = inside * (0.8 / diag)
        return diag, c * inside, beta, beta * c

    diag0, mult0, beta0, gamma0 = coefs(c0)
    diag1, mult1, beta1, gamma1 = coefs(c0 * 0.25)
    diag2, mult2, beta2, gamma2 = coefs(c0 * 0.0625)

    def pairs(x, step):
        def f(i):
            return (x(i - 1) + x(i + 1)) + (roll(x(i), step) + roll(x(i), -step))
        return f

    def second(first, gamma, step):
        s = pairs(first, step)
        return memo(lambda i: 1.2 * first(i) + gamma * s(i))

    def sweep(x, first, gamma, step):
        s = pairs(x, step)
        return memo(lambda i: (0.2 * x(i) + first(i)) + gamma * s(i))

    def defect(x, rhs, diag, mult, step):
        s = pairs(x, step)
        return memo(lambda i: (rhs(i) - diag * x(i)) + mult * s(i))

    def restrict(x, step):
        even = (lane // step) % 2 == 0

        def f(i):
            q = x(2 * i) + x(2 * i + 1)
            return 0.25 * (q + jnp.where(even, roll(q, -step), roll(q, step)))
        return memo(f)

    def all_of(f, low, high):
        for i in range(low, high + 1):
            f(i)
        return f

    dep = all_of(memo(load), -26, 57)
    first0 = all_of(memo(lambda i: beta0 * dep(i)), -26, 57)
    x0 = all_of(second(first0, gamma0, 1), -25, 56)
    rhs1 = all_of(restrict(all_of(defect(x0, dep, diag0, mult0, 1), -24, 55), 1), -12, 27)
    first1 = all_of(memo(lambda i: beta1 * rhs1(i)), -12, 27)
    x1 = all_of(second(first1, gamma1, 2), -11, 26)
    rhs2 = all_of(restrict(all_of(defect(x1, rhs1, diag1, mult1, 2), -10, 25), 2), -5, 12)
    first2 = all_of(memo(lambda i: beta2 * rhs2(i)), -5, 12)
    x2 = all_of(second(first2, gamma2, 4), -4, 11)
    x2 = all_of(sweep(x2, first2, gamma2, 4), -3, 10)
    x2 = all_of(sweep(x2, first2, gamma2, 4), -2, 9)
    y1 = all_of(memo(lambda i: x1(i) + x2(i >> 1)), -3, 18)
    y1 = all_of(sweep(y1, first1, gamma1, 2), -2, 17)
    y1 = all_of(sweep(y1, first1, gamma1, 2), -1, 16)
    y0 = all_of(memo(lambda i: x0(i) + y1(i >> 1)), -2, 33)
    y0 = all_of(sweep(y0, first0, gamma0, 1), -1, 32)
    return sweep(y0, first0, gamma0, 1)


def window(rows):
    lane = lane_iota(8)

    def load(i):
        k, hi, r = (i + 32) // 32, (i % 32) // 16, i % 16
        before, here, after = rows(k, r), rows(k, r + 32), rows(k, r + 64)
        if hi == 0:
            sides = roll(jnp.where(lane < 32, after, before), -32)
            return jnp.where((lane >= 32) & (lane < 96), roll(here, 32), sides)
        sides = roll(jnp.where(lane < 96, after, before), 32)
        return jnp.where((lane >= 32) & (lane < 96), roll(here, -32), sides)

    return load


def inside_of(g):
    chunk, lane = sub_iota() // 2, lane_iota(8)
    out = ((g == 0) & (chunk == 0) & (lane < 32)) | ((g == NLATDEV - 1) & (chunk == 3) & (lane >= 96))
    return jnp.where(out, 0.0, 1.0)


def cycle_kernel(ext, helm, out, rows):
    g = lax.axis_index("lat")
    lev = sub_iota() % 2
    c0 = jnp.where(lev == 0, jnp.full((8, LANES), helm[0], jnp.float32), jnp.full((8, LANES), helm[1], jnp.float32))
    result = v_cycle(window(lambda k, at: ext[k, pl.ds(at, 8, stride=16), :]), c0, inside_of(g))
    for i in range(32):
        rows[8 * i:8 * i + 8, :] = result(i)
    low = lane_iota(8) < 64
    for block in range(4):
        for lev in range(2):
            for pair in range(2):
                left = rows[pl.ds(64 * block + 4 * pair + lev, 8, stride=8), :]
                right = rows[pl.ds(64 * block + 4 * pair + 2 + lev, 8, stride=8), :]
                out[lev, 8 * block:8 * block + 8, 128 * pair:128 * pair + 128] = jnp.where(
                    low, roll(left, -32), roll(right, 32))


def per_device(field, offsets, fraction, helm):
    vmem = pl.BlockSpec(memory_space=pltpu.VMEM)
    smem = pl.BlockSpec(memory_space=pltpu.SMEM)
    hbm = pl.BlockSpec(memory_space=pltpu.HBM)
    parts = pltpu.VMEM((REP, 2 * OWNERS, LANES), jnp.float32)
    circles = pltpu.VMEM((REP, LANES, LANES), jnp.float32)
    ext = pl.pallas_call(
        exchange_kernel,
        out_shape=jax.ShapeDtypeStruct((3, 192, LANES), jnp.float32),
        in_specs=[hbm, hbm, hbm],
        out_specs=vmem,
        scratch_shapes=[
            pltpu.VMEM(field.shape, jnp.float32),
            pltpu.SMEM(offsets.shape, jnp.int32),
            pltpu.SMEM(fraction.shape, jnp.float32),
            parts, circles, circles, parts, circles,
            pltpu.VMEM((2, REP, 2 * OWNERS, LANES), jnp.float32),
            pltpu.SemaphoreType.DMA((3,)),
            pltpu.SemaphoreType.DMA((3 + PLANES,)),
            pltpu.SemaphoreType.DMA((2,)),
            pltpu.SemaphoreType.DMA((2,)),
            pltpu.SemaphoreType.DMA((2, 3)),
            pltpu.SemaphoreType.DMA((2, 3)),
            pltpu.SemaphoreType.REGULAR,
            pltpu.SemaphoreType.REGULAR,
        ],
        compiler_params=pltpu.CompilerParams(collective_id=0, has_side_effects=True, vmem_limit_bytes=16 * 1024 * 1024),
    )(*(pltpu.with_memory_space_constraint(a, pltpu.HBM) for a in (field, offsets, fraction)))
    return pl.pallas_call(
        cycle_kernel,
        out_shape=jax.ShapeDtypeStruct(field.shape, jnp.float32),
        in_specs=[vmem, smem],
        out_specs=vmem,
        scratch_shapes=[pltpu.VMEM((256, LANES), jnp.float32)],
        compiler_params=pltpu.CompilerParams(vmem_limit_bytes=16 * 1024 * 1024),
    )(ext, helm)


def solution(mesh):
    return jax.shard_map(
        per_device,
        mesh=mesh,
        in_specs=(P(None, "lon", "lat"), P("lat"), P("lat"), P()),
        out_specs=P(None, "lon", "lat"),
        check_vma=False,
    )
```

```python
import jax
import jax.numpy as jnp
from jax import lax
from jax.experimental import pallas as pl
from jax.experimental.pallas import tpu as pltpu
from jax.sharding import PartitionSpec as P

MESH = pl.DeviceIdType.MESH
NLONDEV = 64
NLATDEV = 8
FIRST = 0
PLANES = 4
OWNERS = 4 * PLANES
REP = NLONDEV // OWNERS
SPLIT = PLANES + (16 - PLANES) // 2
LANES = 128


def roll(x, shift):
    return pltpu.roll(x, shift % LANES, 1)


def lane_iota(rows):
    return lax.broadcasted_iota(jnp.int32, (rows, LANES), 1)


def sub_iota():
    return lax.broadcasted_iota(jnp.int32, (8, LANES), 0)


def pack_field(half):
    low = lane_iota(16) < 64
    pieces = []
    for chunk in range(4):
        for lev in range(2):
            first, second = half(lev, 0, chunk // 2), half(lev, 1, chunk // 2)
            if chunk % 2 == 0:
                pieces.append(jnp.where(low, first, roll(second, 64)))
            else:
                pieces.append(jnp.where(low, roll(first, 64), second))
    return jnp.concatenate(pieces, axis=0)


def by_chunk(chunk, values, dtype):
    full = jnp.full((8, LANES), values[0], dtype)
    for c in range(1, 4):
        full = jnp.where(chunk == c, jnp.full((8, LANES), values[c], dtype), full)
    return full


def shift_coarse(x, offset):
    v = [x[8 * i:8 * i + 8] for i in range(16)]
    sub = sub_iota()
    for bit in range(7):
        by = 1 << bit
        take = (offset // (16 * by)) % 2 == 1
        if by < 8:
            turned = [pltpu.roll(u, by, 0) for u in v]
            moved = [jnp.where(sub < by, turned[i - 1], turned[i]) for i in range(16)]
        else:
            moved = [v[i - by // 8] for i in range(16)]
        v = [jnp.where(take, m, u) for m, u in zip(moved, v)]
    return jnp.concatenate(v, axis=0)


def shift_fine(v, offset):
    for bit in range(4):
        by = 1 << bit
        take = (offset // by) % 2 == 1
        v = [jnp.where(take, v[r - by] if r >= by else roll(v[r - by + 16], 1), v[r]) for r in range(16)]
    return v


def interpolate(g, s):
    w_one = -s * (s - 1.0) * (s - 2.0) / 6.0
    w_two = (s + 1.0) * (s - 1.0) * (s - 2.0) / 2.0
    w_three = -(s + 1.0) * s * (s - 2.0) / 2.0
    w_four = (s + 1.0) * s * (s - 1.0) / 6.0
    ext = [roll(g[14], 1), roll(g[15], 1)] + g + [roll(g[0], -1)]
    return [w_one * ext[r + 3] + w_two * ext[r + 2] + w_three * ext[r + 1] + w_four * ext[r] for r in range(16)]


def exchange_kernel(field_in, offsets_in, fraction_in, helm_in, ext, coef, field, offsets, fraction, helm, send1, recv1, send2, recv2, work,
                    beside,
                    load_sems, sems, beside_send, beside_recv, near_send, near_recv, lat_in, may_near):
    d = lax.axis_index("lon")
    g = lax.axis_index("lat")
    north, south = g > 0, g < NLATDEV - 1
    rank = lax.rem(d + NLONDEV - 4 * FIRST, NLONDEV)
    owner = rank < OWNERS

    loads = [pltpu.make_async_copy(src, dst, load_sems.at[i]) for i, (src, dst) in enumerate(
        ((field_in, field), (offsets_in, offsets), (fraction_in, fraction), (helm_in, helm)))]
    for load in loads:
        load.start()

    barrier = pltpu.get_barrier_semaphore()

    def tell_lat(sem):
        for there, to in ((north, -1), (south, 1)):
            @pl.when(there)
            def _():
                pl.semaphore_signal(sem, inc=1, device_id={"lat": g + to}, device_id_type=MESH)

    @pl.when(owner)
    def _():
        def greet(j, carry):
            to = lax.rem(OWNERS + 4 * FIRST + j, NLONDEV)

            @pl.when(to != d)
            def _():
                pl.semaphore_signal(barrier, inc=1, device_id={"lon": to}, device_id_type=MESH)
            return carry

        tell_lat(barrier)
        lax.fori_loop(0, NLONDEV, greet, 0)

    loads[0].wait()
    packed = pack_field(lambda lev, hi, pair: field[lev, 16 * hi:16 * hi + 16, 128 * pair:128 * pair + 128]).T
    for hi in range(2):
        for s in range(REP):
            at = 64 * hi + OWNERS * s
            send1[s, pl.ds(hi, OWNERS, stride=2), :] = packed[at:at + OWNERS]

    one = owner.astype(jnp.int32)
    sides = north.astype(jnp.int32) + south.astype(jnp.int32)
    pl.semaphore_wait(barrier, OWNERS - one + one * sides)
    mine, ranked = pl.ds(2 * d, 2), pl.ds(2 * rank, 2)

    def collect(j, carry):
        to_rank = lax.rem(rank + j, OWNERS)
        to = lax.rem(to_rank + 4 * FIRST, NLONDEV)
        pltpu.make_async_remote_copy(
            src_ref=send1.at[:, pl.ds(2 * to_rank, 2)], dst_ref=recv1.at[:, mine],
            send_sem=sems.at[0], recv_sem=sems.at[1],
            device_id={"lon": to}, device_id_type=MESH,
        ).start()
        return carry

    lax.fori_loop(one, OWNERS, collect, 0)
    for load in loads[1:]:
        load.wait()
    coef[...] = jnp.where(sub_iota() % 2 == 0, jnp.full((8, LANES), helm[0], jnp.float32),
                          jnp.full((8, LANES), helm[1], jnp.float32))

    @pl.when(owner)
    def _():
        pltpu.make_async_copy(send1.at[:, ranked], recv1.at[:, mine], sems.at[1]).start()
        pltpu.make_async_copy(recv1, recv1, sems.at[1]).wait()
        tell_lat(lat_in)
        for s in range(REP):
            own = [rank + OWNERS * s + 64 * c for c in range(4)]
            turns = [offsets[i] for i in own]
            work[s] = shift_coarse(recv1[s], by_chunk(lane_iota(8) // 32, turns, jnp.int32)).T
            v = [work[s, pl.ds(r, 8, stride=16), :] for r in range(16)]
            v = shift_fine(v, by_chunk(sub_iota() // 2, turns, jnp.int32))
            v = interpolate(v, by_chunk(sub_iota() // 2, [fraction[i] for i in own], jnp.float32))
            for r in range(16):
                work[s, pl.ds(r, 8, stride=16), :] = v[r]
            send2[s] = work[s].T

        def spread(j, carry):
            k = j // 4
            far = k - PLANES - 1
            plane = jnp.where(far % 2 == 0, PLANES + far // 2, SPLIT + far // 2)
            plane = jnp.where(k == 0, 15, jnp.where(far < 0, k - 1, plane))
            to = lax.rem(4 * (plane + FIRST) + lax.rem(j + d, 4), NLONDEV)

            @pl.when(to != d)
            def _():
                pltpu.make_async_remote_copy(
                    src_ref=send2.at[:, pl.ds(2 * to, 2)], dst_ref=recv2.at[:, ranked],
                    send_sem=sems.at[2], recv_sem=sems.at[3 + rank // 4],
                    device_id={"lon": to}, device_id_type=MESH,
                ).start()
            return carry

        lax.fori_loop(0, NLONDEV, spread, 0)
        pltpu.make_async_copy(send2.at[:, mine], recv2.at[:, ranked], sems.at[3 + rank // 4]).start()
        pl.semaphore_wait(lat_in, sides)
        for i in range(OWNERS, NLONDEV, OWNERS):
            pl.semaphore_signal(may_near, inc=1, device_id={"lon": lax.rem(d + i, NLONDEV)}, device_id_type=MESH)

    falling = (rank >= OWNERS) & (rank < 4 * SPLIT)
    for k in range(PLANES):
        p = jnp.where(falling, PLANES - 1 - k, k)
        part = recv2.at[:, pl.ds(pl.multiple_of(8 * p, 8), 8)]
        pltpu.make_async_copy(part, part, sems.at[3 + p]).wait()
        for side, dd in ((0, 1), (1, -1)):
            pltpu.make_async_remote_copy(
                src_ref=part, dst_ref=beside.at[side, :, pl.ds(pl.multiple_of(8 * p, 8), 8)],
                send_sem=beside_send.at[side], recv_sem=beside_recv.at[side],
                device_id={"lon": lax.rem(d + dd + NLONDEV, NLONDEV)}, device_id_type=MESH,
            ).start()

    def turned(rows):
        return jnp.concatenate(
            [rows[s, pl.ds(hi, OWNERS, stride=2), :] for hi in range(2) for s in range(REP)], axis=0).T

    ext[1, 32:160, :] = turned(recv2)

    def near(dd, to):
        if to < 0:
            src, dst = ext.at[1, pl.ds(32, 32)], ext.at[1 - dd, pl.ds(160, 32)]
        else:
            src, dst = ext.at[1, pl.ds(128, 32)], ext.at[1 - dd, pl.ds(0, 32)]
        return pltpu.make_async_remote_copy(
            src_ref=src, dst_ref=dst,
            send_sem=near_send.at[(to + 1) // 2, dd + 1], recv_sem=near_recv.at[(to + 1) // 2, dd + 1],
            device_id={"lon": lax.rem(d + dd + NLONDEV, NLONDEV), "lat": g + to},
            device_id_type=MESH)

    @pl.when(jnp.logical_not(owner))
    def _():
        pl.semaphore_wait(may_near, 1)

    for there, to in ((north, -1), (south, 1)):
        @pl.when(there)
        def _():
            for dd in (-1, 0, 1):
                near(dd, to).start()
    for edge, at in ((north, 0), (south, 160)):
        @pl.when(jnp.logical_not(edge))
        def _():
            for k in range(3):
                ext[k, at:at + 32, :] = jnp.zeros((32, LANES), jnp.float32)

    for side in range(2):
        pltpu.make_async_copy(beside.at[side], beside.at[side], beside_recv.at[side]).wait()
        ext[2 * side, 32:160, :] = turned(beside.at[side])
        pltpu.make_async_copy(recv2, recv2, beside_send.at[side]).wait()
    for there, to in ((north, -1), (south, 1)):
        @pl.when(there)
        def _():
            for dd in (-1, 0, 1):
                near(dd, to).wait_send()
                near(dd, -to).wait_recv()

    @pl.when(owner)
    def _():
        for src, i in ((send1, 0), (send2, 2)):
            part = src.at[:, pl.ds(0, src.shape[1] - 2)]
            pltpu.make_async_copy(part, part, sems.at[i]).wait()

    @pl.when(jnp.logical_not(owner))
    def _():
        pltpu.make_async_copy(send1, send1, sems.at[0]).wait()


def memo(f):
    seen = {}

    def g(i):
        if i not in seen:
            seen[i] = f(i)
        return seen[i]

    return g


def v_cycle(load, c0, inside):
    lane = lane_iota(8)

    def coefs(c):
        diag = 1.0 + 4.0 * c
        beta = inside * (0.8 / diag)
        return diag, c * inside, beta, beta * c

    diag0, mult0, beta0, gamma0 = coefs(c0)
    diag1, mult1, beta1, gamma1 = coefs(c0 * 0.25)
    diag2, mult2, beta2, gamma2 = coefs(c0 * 0.0625)

    def pairs(x, step):
        def f(i):
            return (x(i - 1) + x(i + 1)) + (roll(x(i), step) + roll(x(i), -step))
        return f

    def second(first, gamma, step):
        s = pairs(first, step)
        return memo(lambda i: 1.2 * first(i) + gamma * s(i))

    def sweep(x, first, gamma, step):
        s = pairs(x, step)
        return memo(lambda i: (0.2 * x(i) + first(i)) + gamma * s(i))

    def defect(x, rhs, diag, mult, step):
        s = pairs(x, step)
        return memo(lambda i: (rhs(i) - diag * x(i)) + mult * s(i))

    def restrict(x, step):
        even = (lane // step) % 2 == 0

        def f(i):
            q = x(2 * i) + x(2 * i + 1)
            return 0.25 * (q + jnp.where(even, roll(q, -step), roll(q, step)))
        return memo(f)

    def all_of(f, low, high):
        for i in range(low, high + 1):
            f(i)
        return f

    dep = all_of(memo(load), -26, 57)
    first0 = all_of(memo(lambda i: beta0 * dep(i)), -26, 57)
    x0 = all_of(second(first0, gamma0, 1), -25, 56)
    rhs1 = all_of(restrict(all_of(defect(x0, dep, diag0, mult0, 1), -24, 55), 1), -12, 27)
    first1 = all_of(memo(lambda i: beta1 * rhs1(i)), -12, 27)
    x1 = all_of(second(first1, gamma1, 2), -11, 26)
    rhs2 = all_of(restrict(all_of(defect(x1, rhs1, diag1, mult1, 2), -10, 25), 2), -5, 12)
    first2 = all_of(memo(lambda i: beta2 * rhs2(i)), -5, 12)
    x2 = all_of(second(first2, gamma2, 4), -4, 11)
    x2 = all_of(sweep(x2, first2, gamma2, 4), -3, 10)
    x2 = all_of(sweep(x2, first2, gamma2, 4), -2, 9)
    y1 = all_of(memo(lambda i: x1(i) + x2(i >> 1)), -3, 18)
    y1 = all_of(sweep(y1, first1, gamma1, 2), -2, 17)
    y1 = all_of(sweep(y1, first1, gamma1, 2), -1, 16)
    y0 = all_of(memo(lambda i: x0(i) + y1(i >> 1)), -2, 33)
    y0 = all_of(sweep(y0, first0, gamma0, 1), -1, 32)
    return sweep(y0, first0, gamma0, 1)


def window(rows):
    lane = lane_iota(8)

    def load(i):
        k, hi, r = (i + 32) // 32, (i % 32) // 16, i % 16
        before, here, after = rows(k, r), rows(k, r + 32), rows(k, r + 64)
        if hi == 0:
            sides = roll(jnp.where(lane < 32, after, before), -32)
            return jnp.where((lane >= 32) & (lane < 96), roll(here, 32), sides)
        sides = roll(jnp.where(lane < 96, after, before), 32)
        return jnp.where((lane >= 32) & (lane < 96), roll(here, -32), sides)

    return load


def inside_of(g):
    chunk, lane = sub_iota() // 2, lane_iota(8)
    out = ((g == 0) & (chunk == 0) & (lane < 32)) | ((g == NLATDEV - 1) & (chunk == 3) & (lane >= 96))
    return jnp.where(out, 0.0, 1.0)


def cycle_kernel(ext, coef, out, rows, block, sems):
    g = lax.axis_index("lat")
    result = v_cycle(window(lambda k, at: ext[k, pl.ds(at, 8, stride=16), :]), coef[...], inside_of(g))
    low = lane_iota(8) < 64
    copies = []
    for b in range(4):
        for i in range(8 * b, 8 * b + 8):
            rows[8 * i:8 * i + 8, :] = result(i)
        for lev in range(2):
            for pair in range(2):
                left = rows[pl.ds(64 * b + 4 * pair + lev, 8, stride=8), :]
                right = rows[pl.ds(64 * b + 4 * pair + 2 + lev, 8, stride=8), :]
                block[lev, 8 * b:8 * b + 8, 128 * pair:128 * pair + 128] = jnp.where(
                    low, roll(left, -32), roll(right, 32))
        part = (slice(None), pl.ds(8 * b, 8))
        copies.append(pltpu.make_async_copy(block.at[part], out.at[part], sems.at[b]))
        copies[-1].start()
    for copy in copies:
        copy.wait()


def per_device(field, offsets, fraction, helm):
    vmem = pl.BlockSpec(memory_space=pltpu.VMEM)
    hbm = pl.BlockSpec(memory_space=pltpu.HBM)
    parts = pltpu.VMEM((REP, 2 * OWNERS, LANES), jnp.float32)
    circles = pltpu.VMEM((REP, LANES, LANES), jnp.float32)
    inputs = [pltpu.with_memory_space_constraint(a, pltpu.HBM) for a in (field, offsets, fraction, helm)]
    ext, coef = pl.pallas_call(
        exchange_kernel,
        out_shape=(jax.ShapeDtypeStruct((3, 192, LANES), jnp.float32), jax.ShapeDtypeStruct((8, LANES), jnp.float32)),
        in_specs=[hbm] * 4,
        out_specs=(vmem, vmem),
        scratch_shapes=[
            pltpu.VMEM(field.shape, jnp.float32),
            pltpu.SMEM(offsets.shape, jnp.int32),
            pltpu.SMEM(fraction.shape, jnp.float32),
            pltpu.SMEM(helm.shape, jnp.float32),
            parts, circles, circles, parts, circles,
            pltpu.VMEM((2, REP, 2 * OWNERS, LANES), jnp.float32),
            pltpu.SemaphoreType.DMA((4,)),
            pltpu.SemaphoreType.DMA((3 + PLANES,)),
            pltpu.SemaphoreType.DMA((2,)),
            pltpu.SemaphoreType.DMA((2,)),
            pltpu.SemaphoreType.DMA((2, 3)),
            pltpu.SemaphoreType.DMA((2, 3)),
            pltpu.SemaphoreType.REGULAR,
            pltpu.SemaphoreType.REGULAR,
        ],
        compiler_params=pltpu.CompilerParams(collective_id=0, has_side_effects=True, vmem_limit_bytes=16 * 1024 * 1024),
    )(*inputs)
    return pl.pallas_call(
        cycle_kernel,
        out_shape=jax.ShapeDtypeStruct(field.shape, jnp.float32),
        in_specs=[vmem, vmem],
        out_specs=hbm,
        scratch_shapes=[
            pltpu.VMEM((256, LANES), jnp.float32),
            pltpu.VMEM(field.shape, jnp.float32),
            pltpu.SemaphoreType.DMA((4,)),
        ],
        compiler_params=pltpu.CompilerParams(vmem_limit_bytes=16 * 1024 * 1024),
    )(ext, coef)


def solution(mesh):
    return jax.shard_map(
        per_device,
        mesh=mesh,
        in_specs=(P(None, "lon", "lat"), P("lat"), P("lat"), P()),
        out_specs=P(None, "lon", "lat"),
        check_vma=False,
    )
```

```python
import jax
import jax.numpy as jnp
from jax import lax
from jax.experimental import pallas as pl
from jax.experimental.pallas import tpu as pltpu
from jax.sharding import PartitionSpec as P

MESH = pl.DeviceIdType.MESH
NLONDEV = 64
NLATDEV = 8
FIRST = 0
PLANES = 4
OWNERS = 4 * PLANES
REP = NLONDEV // OWNERS
SERVED = (15, 4, 0, 5, 1, 6, 2, 7, 3, 8, 9, 10, 11, 12, 13, 14)
SPLIT = PLANES + (16 - PLANES) // 2
LANES = 128


def roll(x, shift):
    return pltpu.roll(x, shift % LANES, 1)


def lane_iota(rows):
    return lax.broadcasted_iota(jnp.int32, (rows, LANES), 1)


def sub_iota():
    return lax.broadcasted_iota(jnp.int32, (8, LANES), 0)


def pack_field(half):
    low = lane_iota(16) < 64
    pieces = []
    for chunk in range(4):
        for lev in range(2):
            first, second = half(lev, 0, chunk // 2), half(lev, 1, chunk // 2)
            if chunk % 2 == 0:
                pieces.append(jnp.where(low, first, roll(second, 64)))
            else:
                pieces.append(jnp.where(low, roll(first, 64), second))
    return jnp.concatenate(pieces, axis=0)


def by_chunk(chunk, values, dtype):
    full = jnp.full((8, LANES), values[0], dtype)
    for c in range(1, 4):
        full = jnp.where(chunk == c, jnp.full((8, LANES), values[c], dtype), full)
    return full


def shift_coarse(x, offset):
    v = [x[8 * i:8 * i + 8] for i in range(16)]
    sub = sub_iota()
    for bit in range(7):
        by = 1 << bit
        take = (offset // (16 * by)) % 2 == 1
        if by < 8:
            turned = [pltpu.roll(u, by, 0) for u in v]
            moved = [jnp.where(sub < by, turned[i - 1], turned[i]) for i in range(16)]
        else:
            moved = [v[i - by // 8] for i in range(16)]
        v = [jnp.where(take, m, u) for m, u in zip(moved, v)]
    return jnp.concatenate(v, axis=0)


def shift_fine(v, offset):
    for bit in range(4):
        by = 1 << bit
        take = (offset // by) % 2 == 1
        v = [jnp.where(take, v[r - by] if r >= by else roll(v[r - by + 16], 1), v[r]) for r in range(16)]
    return v


def interpolate(g, s):
    w_one = -s * (s - 1.0) * (s - 2.0) / 6.0
    w_two = (s + 1.0) * (s - 1.0) * (s - 2.0) / 2.0
    w_three = -(s + 1.0) * s * (s - 2.0) / 2.0
    w_four = (s + 1.0) * s * (s - 1.0) / 6.0
    ext = [roll(g[14], 1), roll(g[15], 1)] + g + [roll(g[0], -1)]
    return [w_one * ext[r + 3] + w_two * ext[r + 2] + w_three * ext[r + 1] + w_four * ext[r] for r in range(16)]


def exchange_kernel(field_in, offsets_in, fraction_in, helm_in, ext, coef, field, offsets, fraction, helm, send1, recv1, send2, recv2, work,
                    beside,
                    load_sems, sems, beside_send, beside_recv, near_send, near_recv, lat_in, may_near):
    d = lax.axis_index("lon")
    g = lax.axis_index("lat")
    north, south = g > 0, g < NLATDEV - 1
    rank = lax.rem(d + NLONDEV - 4 * FIRST, NLONDEV)
    owner = rank < OWNERS

    parts = [(lev, pl.ds(16 * hi, 16)) for lev in range(2) for hi in range(2)]
    loads = [pltpu.make_async_copy(src, dst, load_sems.at[i]) for i, (src, dst) in enumerate(
        [(field_in.at[at], field.at[at]) for at in parts]
        + [(offsets_in, offsets), (fraction_in, fraction), (helm_in, helm)])]
    for load in loads:
        load.start()

    barrier = pltpu.get_barrier_semaphore()

    def tell_lat(sem):
        for there, to in ((north, -1), (south, 1)):
            @pl.when(there)
            def _():
                pl.semaphore_signal(sem, inc=1, device_id={"lat": g + to}, device_id_type=MESH)

    @pl.when(owner)
    def _():
        def greet(j, carry):
            to = lax.rem(OWNERS + 4 * FIRST + j, NLONDEV)

            @pl.when(to != d)
            def _():
                pl.semaphore_signal(barrier, inc=1, device_id={"lon": to}, device_id_type=MESH)
            return carry

        tell_lat(barrier)
        lax.fori_loop(0, NLONDEV, greet, 0)

    for load in loads[:4]:
        load.wait()
    packed = pack_field(lambda lev, hi, pair: field[lev, 16 * hi:16 * hi + 16, 128 * pair:128 * pair + 128]).T
    for hi in range(2):
        for s in range(REP):
            at = 64 * hi + OWNERS * s
            send1[s, pl.ds(hi, OWNERS, stride=2), :] = packed[at:at + OWNERS]

    one = owner.astype(jnp.int32)
    sides = north.astype(jnp.int32) + south.astype(jnp.int32)
    pl.semaphore_wait(barrier, OWNERS - one + one * sides)
    mine, ranked = pl.ds(2 * d, 2), pl.ds(2 * rank, 2)

    def collect(j, carry):
        k = j // 4
        farthest = 4 * jnp.where(d >= 40, PLANES - 1 - k, k) + lax.rem(j + d, 4)
        to_rank = jnp.where(owner, lax.rem(rank + j, OWNERS), farthest)
        to = lax.rem(to_rank + 4 * FIRST, NLONDEV)
        pltpu.make_async_remote_copy(
            src_ref=send1.at[:, pl.ds(2 * to_rank, 2)], dst_ref=recv1.at[:, mine],
            send_sem=sems.at[0], recv_sem=sems.at[1],
            device_id={"lon": to}, device_id_type=MESH,
        ).start()
        return carry

    lax.fori_loop(one, OWNERS, collect, 0)
    for load in loads[4:]:
        load.wait()
    coef[...] = jnp.where(sub_iota() % 2 == 0, jnp.full((8, LANES), helm[0], jnp.float32),
                          jnp.full((8, LANES), helm[1], jnp.float32))

    @pl.when(owner)
    def _():
        pltpu.make_async_copy(send1.at[:, ranked], recv1.at[:, mine], sems.at[1]).start()
        pltpu.make_async_copy(recv1, recv1, sems.at[1]).wait()
        tell_lat(lat_in)
        for s in range(REP):
            own = [rank + OWNERS * s + 64 * c for c in range(4)]
            turns = [offsets[i] for i in own]
            work[s] = shift_coarse(recv1[s], by_chunk(lane_iota(8) // 32, turns, jnp.int32)).T
            v = [work[s, pl.ds(r, 8, stride=16), :] for r in range(16)]
            v = shift_fine(v, by_chunk(sub_iota() // 2, turns, jnp.int32))
            v = interpolate(v, by_chunk(sub_iota() // 2, [fraction[i] for i in own], jnp.float32))
            for r in range(16):
                work[s, pl.ds(r, 8, stride=16), :] = v[r]
            send2[s] = work[s].T

        for plane in SERVED:
            def spread(j, carry):
                to = 4 * plane + lax.rem(j + d, 4)

                @pl.when(to != d)
                def _():
                    pltpu.make_async_remote_copy(
                        src_ref=send2.at[:, pl.ds(2 * to, 2)], dst_ref=recv2.at[:, ranked],
                        send_sem=sems.at[2], recv_sem=sems.at[3 + rank // 4],
                        device_id={"lon": to}, device_id_type=MESH,
                    ).start()
                return carry

            lax.fori_loop(0, 4, spread, 0)

        pltpu.make_async_copy(send2.at[:, mine], recv2.at[:, ranked], sems.at[3 + rank // 4]).start()
        pl.semaphore_wait(lat_in, sides)
        for i in range(OWNERS, NLONDEV, OWNERS):
            pl.semaphore_signal(may_near, inc=1, device_id={"lon": lax.rem(d + i, NLONDEV)}, device_id_type=MESH)

    falling = (rank >= OWNERS) & (rank < 4 * SPLIT)
    for k in range(PLANES):
        p = jnp.where(falling, PLANES - 1 - k, k)
        part = recv2.at[:, pl.ds(pl.multiple_of(8 * p, 8), 8)]
        pltpu.make_async_copy(part, part, sems.at[3 + p]).wait()
        for side, dd in ((0, 1), (1, -1)):
            pltpu.make_async_remote_copy(
                src_ref=part, dst_ref=beside.at[side, :, pl.ds(pl.multiple_of(8 * p, 8), 8)],
                send_sem=beside_send.at[side], recv_sem=beside_recv.at[side],
                device_id={"lon": lax.rem(d + dd + NLONDEV, NLONDEV)}, device_id_type=MESH,
            ).start()

    def turned(rows):
        return jnp.concatenate(
            [rows[s, pl.ds(hi, OWNERS, stride=2), :] for hi in range(2) for s in range(REP)], axis=0).T

    ext[1, 32:160, :] = turned(recv2)

    def near(dd, to):
        if to < 0:
            src, dst = ext.at[1, pl.ds(32, 32)], ext.at[1 - dd, pl.ds(160, 32)]
        else:
            src, dst = ext.at[1, pl.ds(128, 32)], ext.at[1 - dd, pl.ds(0, 32)]
        return pltpu.make_async_remote_copy(
            src_ref=src, dst_ref=dst,
            send_sem=near_send.at[(to + 1) // 2, dd + 1], recv_sem=near_recv.at[(to + 1) // 2, dd + 1],
            device_id={"lon": lax.rem(d + dd + NLONDEV, NLONDEV), "lat": g + to},
            device_id_type=MESH)

    @pl.when(jnp.logical_not(owner))
    def _():
        pl.semaphore_wait(may_near, 1)

    for there, to in ((north, -1), (south, 1)):
        @pl.when(there)
        def _():
            for dd in (-1, 0, 1):
                near(dd, to).start()
    for edge, at in ((north, 0), (south, 160)):
        @pl.when(jnp.logical_not(edge))
        def _():
            for k in range(3):
                ext[k, at:at + 32, :] = jnp.zeros((32, LANES), jnp.float32)

    for side in range(2):
        pltpu.make_async_copy(beside.at[side], beside.at[side], beside_recv.at[side]).wait()
        ext[2 * side, 32:160, :] = turned(beside.at[side])
        pltpu.make_async_copy(recv2, recv2, beside_send.at[side]).wait()
    for there, to in ((north, -1), (south, 1)):
        @pl.when(there)
        def _():
            for dd in (-1, 0, 1):
                near(dd, to).wait_send()
                near(dd, -to).wait_recv()

    @pl.when(owner)
    def _():
        for src, i in ((send1, 0), (send2, 2)):
            part = src.at[:, pl.ds(0, src.shape[1] - 2)]
            pltpu.make_async_copy(part, part, sems.at[i]).wait()

    @pl.when(jnp.logical_not(owner))
    def _():
        pltpu.make_async_copy(send1, send1, sems.at[0]).wait()


def memo(f):
    seen = {}

    def g(i):
        if i not in seen:
            seen[i] = f(i)
        return seen[i]

    return g


def v_cycle(load, c0, inside):
    lane = lane_iota(8)

    def coefs(c):
        diag = 1.0 + 4.0 * c
        beta = inside * (0.8 / diag)
        return diag, c * inside, beta, beta * c

    diag0, mult0, beta0, gamma0 = coefs(c0)
    diag1, mult1, beta1, gamma1 = coefs(c0 * 0.25)
    diag2, mult2, beta2, gamma2 = coefs(c0 * 0.0625)

    def pairs(x, step):
        def f(i):
            return (x(i - 1) + x(i + 1)) + (roll(x(i), step) + roll(x(i), -step))
        return f

    def second(first, gamma, step):
        s = pairs(first, step)
        return memo(lambda i: 1.2 * first(i) + gamma * s(i))

    def sweep(x, first, gamma, step):
        s = pairs(x, step)
        return memo(lambda i: (0.2 * x(i) + first(i)) + gamma * s(i))

    def defect(x, rhs, diag, mult, step):
        s = pairs(x, step)
        return memo(lambda i: (rhs(i) - diag * x(i)) + mult * s(i))

    def restrict(x, step):
        even = (lane // step) % 2 == 0

        def f(i):
            q = x(2 * i) + x(2 * i + 1)
            return 0.25 * (q + jnp.where(even, roll(q, -step), roll(q, step)))
        return memo(f)

    def all_of(f, low, high):
        for i in range(low, high + 1):
            f(i)
        return f

    dep = all_of(memo(load), -26, 57)
    first0 = all_of(memo(lambda i: beta0 * dep(i)), -26, 57)
    x0 = all_of(second(first0, gamma0, 1), -25, 56)
    rhs1 = all_of(restrict(all_of(defect(x0, dep, diag0, mult0, 1), -24, 55), 1), -12, 27)
    first1 = all_of(memo(lambda i: beta1 * rhs1(i)), -12, 27)
    x1 = all_of(second(first1, gamma1, 2), -11, 26)
    rhs2 = all_of(restrict(all_of(defect(x1, rhs1, diag1, mult1, 2), -10, 25), 2), -5, 12)
    first2 = all_of(memo(lambda i: beta2 * rhs2(i)), -5, 12)
    x2 = all_of(second(first2, gamma2, 4), -4, 11)
    x2 = all_of(sweep(x2, first2, gamma2, 4), -3, 10)
    x2 = all_of(sweep(x2, first2, gamma2, 4), -2, 9)
    y1 = all_of(memo(lambda i: x1(i) + x2(i >> 1)), -3, 18)
    y1 = all_of(sweep(y1, first1, gamma1, 2), -2, 17)
    y1 = all_of(sweep(y1, first1, gamma1, 2), -1, 16)
    y0 = all_of(memo(lambda i: x0(i) + y1(i >> 1)), -2, 33)
    y0 = all_of(sweep(y0, first0, gamma0, 1), -1, 32)
    return sweep(y0, first0, gamma0, 1)


def window(rows):
    lane = lane_iota(8)

    def load(i):
        k, hi, r = (i + 32) // 32, (i % 32) // 16, i % 16
        before, here, after = rows(k, r), rows(k, r + 32), rows(k, r + 64)
        if hi == 0:
            sides = roll(jnp.where(lane < 32, after, before), -32)
            return jnp.where((lane >= 32) & (lane < 96), roll(here, 32), sides)
        sides = roll(jnp.where(lane < 96, after, before), 32)
        return jnp.where((lane >= 32) & (lane < 96), roll(here, -32), sides)

    return load


def inside_of(g):
    chunk, lane = sub_iota() // 2, lane_iota(8)
    out = ((g == 0) & (chunk == 0) & (lane < 32)) | ((g == NLATDEV - 1) & (chunk == 3) & (lane >= 96))
    return jnp.where(out, 0.0, 1.0)


def cycle_kernel(ext, coef, out, rows, block, sems):
    g = lax.axis_index("lat")
    result = v_cycle(window(lambda k, at: ext[k, pl.ds(at, 8, stride=16), :]), coef[...], inside_of(g))
    low = lane_iota(8) < 64
    copies = []
    for b in range(4):
        for i in range(8 * b, 8 * b + 8):
            rows[8 * i:8 * i + 8, :] = result(i)
        for lev in range(2):
            for pair in range(2):
                left = rows[pl.ds(64 * b + 4 * pair + lev, 8, stride=8), :]
                right = rows[pl.ds(64 * b + 4 * pair + 2 + lev, 8, stride=8), :]
                block[lev, 8 * b:8 * b + 8, 128 * pair:128 * pair + 128] = jnp.where(
                    low, roll(left, -32), roll(right, 32))
        part = (slice(None), pl.ds(8 * b, 8))
        copies.append(pltpu.make_async_copy(block.at[part], out.at[part], sems.at[b]))
        copies[-1].start()
    for copy in copies:
        copy.wait()


def per_device(field, offsets, fraction, helm):
    vmem = pl.BlockSpec(memory_space=pltpu.VMEM)
    hbm = pl.BlockSpec(memory_space=pltpu.HBM)
    parts = pltpu.VMEM((REP, 2 * OWNERS, LANES), jnp.float32)
    circles = pltpu.VMEM((REP, LANES, LANES), jnp.float32)
    inputs = [pltpu.with_memory_space_constraint(a, pltpu.HBM) for a in (field, offsets, fraction, helm)]
    ext, coef = pl.pallas_call(
        exchange_kernel,
        out_shape=(jax.ShapeDtypeStruct((3, 192, LANES), jnp.float32), jax.ShapeDtypeStruct((8, LANES), jnp.float32)),
        in_specs=[hbm] * 4,
        out_specs=(vmem, vmem),
        scratch_shapes=[
            pltpu.VMEM(field.shape, jnp.float32),
            pltpu.SMEM(offsets.shape, jnp.int32),
            pltpu.SMEM(fraction.shape, jnp.float32),
            pltpu.SMEM(helm.shape, jnp.float32),
            parts, circles, circles, parts, circles,
            pltpu.VMEM((2, REP, 2 * OWNERS, LANES), jnp.float32),
            pltpu.SemaphoreType.DMA((7,)),
            pltpu.SemaphoreType.DMA((3 + PLANES,)),
            pltpu.SemaphoreType.DMA((2,)),
            pltpu.SemaphoreType.DMA((2,)),
            pltpu.SemaphoreType.DMA((2, 3)),
            pltpu.SemaphoreType.DMA((2, 3)),
            pltpu.SemaphoreType.REGULAR,
            pltpu.SemaphoreType.REGULAR,
        ],
        compiler_params=pltpu.CompilerParams(collective_id=0, has_side_effects=True, vmem_limit_bytes=16 * 1024 * 1024),
    )(*inputs)
    return pl.pallas_call(
        cycle_kernel,
        out_shape=jax.ShapeDtypeStruct(field.shape, jnp.float32),
        in_specs=[vmem, vmem],
        out_specs=hbm,
        scratch_shapes=[
            pltpu.VMEM((256, LANES), jnp.float32),
            pltpu.VMEM(field.shape, jnp.float32),
            pltpu.SemaphoreType.DMA((4,)),
        ],
        compiler_params=pltpu.CompilerParams(vmem_limit_bytes=16 * 1024 * 1024),
    )(ext, coef)


def solution(mesh):
    return jax.shard_map(
        per_device,
        mesh=mesh,
        in_specs=(P(None, "lon", "lat"), P("lat"), P("lat"), P()),
        out_specs=P(None, "lon", "lat"),
        check_vma=False,
    )
```

```python
import jax
import jax.numpy as jnp
from jax import lax
from jax.experimental import pallas as pl
from jax.experimental.pallas import tpu as pltpu
from jax.sharding import PartitionSpec as P

MESH = pl.DeviceIdType.MESH
NLONDEV = 64
NLATDEV = 8
FIRST = 0
PLANES = 4
OWNERS = 4 * PLANES
REP = NLONDEV // OWNERS
SERVED = (15, 4, 0, 5, 1, 6, 2, 9, 3, 7, 8, 10, 11, 12, 13, 14)
SPLIT = PLANES + (16 - PLANES) // 2
LANES = 128


def roll(x, shift):
    return pltpu.roll(x, shift % LANES, 1)


def lane_iota(rows):
    return lax.broadcasted_iota(jnp.int32, (rows, LANES), 1)


def sub_iota():
    return lax.broadcasted_iota(jnp.int32, (8, LANES), 0)


def pack_field(half):
    low = lane_iota(16) < 64
    pieces = []
    for chunk in range(4):
        for lev in range(2):
            first, second = half(lev, 0, chunk // 2), half(lev, 1, chunk // 2)
            if chunk % 2 == 0:
                pieces.append(jnp.where(low, first, roll(second, 64)))
            else:
                pieces.append(jnp.where(low, roll(first, 64), second))
    return jnp.concatenate(pieces, axis=0)


def by_chunk(chunk, values, dtype):
    full = jnp.full((8, LANES), values[0], dtype)
    for c in range(1, 4):
        full = jnp.where(chunk == c, jnp.full((8, LANES), values[c], dtype), full)
    return full


def shift_coarse(x, offset):
    v = [x[8 * i:8 * i + 8] for i in range(16)]
    sub = sub_iota()
    for bit in range(7):
        by = 1 << bit
        take = (offset // (16 * by)) % 2 == 1
        if by < 8:
            turned = [pltpu.roll(u, by, 0) for u in v]
            moved = [jnp.where(sub < by, turned[i - 1], turned[i]) for i in range(16)]
        else:
            moved = [v[i - by // 8] for i in range(16)]
        v = [jnp.where(take, m, u) for m, u in zip(moved, v)]
    return jnp.concatenate(v, axis=0)


def shift_fine(v, offset):
    for bit in range(4):
        by = 1 << bit
        take = (offset // by) % 2 == 1
        v = [jnp.where(take, v[r - by] if r >= by else roll(v[r - by + 16], 1), v[r]) for r in range(16)]
    return v


def interpolate(g, s):
    w_one = -s * (s - 1.0) * (s - 2.0) / 6.0
    w_two = (s + 1.0) * (s - 1.0) * (s - 2.0) / 2.0
    w_three = -(s + 1.0) * s * (s - 2.0) / 2.0
    w_four = (s + 1.0) * s * (s - 1.0) / 6.0
    ext = [roll(g[14], 1), roll(g[15], 1)] + g + [roll(g[0], -1)]
    return [w_one * ext[r + 3] + w_two * ext[r + 2] + w_three * ext[r + 1] + w_four * ext[r] for r in range(16)]


def exchange_kernel(field_in, offsets_in, fraction_in, helm_in, ext, coef, field, offsets, fraction, helm, send1, recv1, send2, recv2, work,
                    beside,
                    load_sems, sems, beside_send, beside_recv, near_send, near_recv, lat_in, may_near):
    d = lax.axis_index("lon")
    g = lax.axis_index("lat")
    north, south = g > 0, g < NLATDEV - 1
    rank = lax.rem(d + NLONDEV - 4 * FIRST, NLONDEV)
    owner = rank < OWNERS

    parts = [(lev, pl.ds(16 * hi, 16)) for lev in range(2) for hi in range(2)]
    loads = [pltpu.make_async_copy(src, dst, load_sems.at[i]) for i, (src, dst) in enumerate(
        [(field_in.at[at], field.at[at]) for at in parts]
        + [(offsets_in, offsets), (fraction_in, fraction), (helm_in, helm)])]
    for load in loads:
        load.start()

    barrier = pltpu.get_barrier_semaphore()

    def tell_lat(sem):
        for there, to in ((north, -1), (south, 1)):
            @pl.when(there)
            def _():
                pl.semaphore_signal(sem, inc=1, device_id={"lat": g + to}, device_id_type=MESH)

    @pl.when(owner)
    def _():
        def greet(j, carry):
            to = lax.rem(OWNERS + 4 * FIRST + j, NLONDEV)

            @pl.when(to != d)
            def _():
                pl.semaphore_signal(barrier, inc=1, device_id={"lon": to}, device_id_type=MESH)
            return carry

        tell_lat(barrier)
        lax.fori_loop(0, NLONDEV, greet, 0)

    for load in loads[:4]:
        load.wait()
    packed = pack_field(lambda lev, hi, pair: field[lev, 16 * hi:16 * hi + 16, 128 * pair:128 * pair + 128]).T
    for hi in range(2):
        for s in range(REP):
            at = 64 * hi + OWNERS * s
            send1[s, pl.ds(hi, OWNERS, stride=2), :] = packed[at:at + OWNERS]

    one = owner.astype(jnp.int32)
    sides = north.astype(jnp.int32) + south.astype(jnp.int32)
    pl.semaphore_wait(barrier, OWNERS - one + one * sides)
    mine, ranked = pl.ds(2 * d, 2), pl.ds(2 * rank, 2)

    def collect(j, carry):
        k = j // 4
        farthest = 4 * jnp.where(d >= 40, PLANES - 1 - k, k) + lax.rem(j + d, 4)
        to_rank = jnp.where(owner, lax.rem(rank + j, OWNERS), farthest)
        to = lax.rem(to_rank + 4 * FIRST, NLONDEV)
        pltpu.make_async_remote_copy(
            src_ref=send1.at[:, pl.ds(2 * to_rank, 2)], dst_ref=recv1.at[:, mine],
            send_sem=sems.at[0], recv_sem=sems.at[1],
            device_id={"lon": to}, device_id_type=MESH,
        ).start()
        return carry

    lax.fori_loop(one, OWNERS, collect, 0)
    for load in loads[4:]:
        load.wait()
    coef[...] = jnp.where(sub_iota() % 2 == 0, jnp.full((8, LANES), helm[0], jnp.float32),
                          jnp.full((8, LANES), helm[1], jnp.float32))

    @pl.when(owner)
    def _():
        pltpu.make_async_copy(send1.at[:, ranked], recv1.at[:, mine], sems.at[1]).start()
        pltpu.make_async_copy(recv1, recv1, sems.at[1]).wait()
        tell_lat(lat_in)
        for s in range(REP):
            own = [rank + OWNERS * s + 64 * c for c in range(4)]
            turns = [offsets[i] for i in own]
            work[s] = shift_coarse(recv1[s], by_chunk(lane_iota(8) // 32, turns, jnp.int32)).T
            v = [work[s, pl.ds(r, 8, stride=16), :] for r in range(16)]
            v = shift_fine(v, by_chunk(sub_iota() // 2, turns, jnp.int32))
            v = interpolate(v, by_chunk(sub_iota() // 2, [fraction[i] for i in own], jnp.float32))
            for r in range(16):
                work[s, pl.ds(r, 8, stride=16), :] = v[r]
            send2[s] = work[s].T

        for plane in SERVED:
            def spread(j, carry):
                to = 4 * plane + lax.rem(j + d, 4)

                @pl.when(to != d)
                def _():
                    pltpu.make_async_remote_copy(
                        src_ref=send2.at[:, pl.ds(2 * to, 2)], dst_ref=recv2.at[:, ranked],
                        send_sem=sems.at[2], recv_sem=sems.at[3 + rank // 4],
                        device_id={"lon": to}, device_id_type=MESH,
                    ).start()
                return carry

            lax.fori_loop(0, 4, spread, 0)

        pltpu.make_async_copy(send2.at[:, mine], recv2.at[:, ranked], sems.at[3 + rank // 4]).start()
        pl.semaphore_wait(lat_in, sides)
        for i in range(OWNERS, NLONDEV, OWNERS):
            pl.semaphore_signal(may_near, inc=1, device_id={"lon": lax.rem(d + i, NLONDEV)}, device_id_type=MESH)

    falling = (rank >= OWNERS) & (rank < 4 * SPLIT)
    for k in range(PLANES):
        p = jnp.where(falling, PLANES - 1 - k, k)
        part = recv2.at[:, pl.ds(pl.multiple_of(8 * p, 8), 8)]
        pltpu.make_async_copy(part, part, sems.at[3 + p]).wait()
        for side, dd in ((0, 1), (1, -1)):
            pltpu.make_async_remote_copy(
                src_ref=part, dst_ref=beside.at[side, :, pl.ds(pl.multiple_of(8 * p, 8), 8)],
                send_sem=beside_send.at[side], recv_sem=beside_recv.at[side],
                device_id={"lon": lax.rem(d + dd + NLONDEV, NLONDEV)}, device_id_type=MESH,
            ).start()

    def turned(rows):
        return jnp.concatenate(
            [rows[s, pl.ds(hi, OWNERS, stride=2), :] for hi in range(2) for s in range(REP)], axis=0).T

    ext[1, 32:160, :] = turned(recv2)

    def near(dd, to):
        if to < 0:
            src, dst = ext.at[1, pl.ds(32, 32)], ext.at[1 - dd, pl.ds(160, 32)]
        else:
            src, dst = ext.at[1, pl.ds(128, 32)], ext.at[1 - dd, pl.ds(0, 32)]
        return pltpu.make_async_remote_copy(
            src_ref=src, dst_ref=dst,
            send_sem=near_send.at[(to + 1) // 2, dd + 1], recv_sem=near_recv.at[(to + 1) // 2, dd + 1],
            device_id={"lon": lax.rem(d + dd + NLONDEV, NLONDEV), "lat": g + to},
            device_id_type=MESH)

    @pl.when(jnp.logical_not(owner))
    def _():
        pl.semaphore_wait(may_near, 1)

    for there, to in ((north, -1), (south, 1)):
        @pl.when(there)
        def _():
            for dd in (-1, 0, 1):
                near(dd, to).start()
    for edge, at in ((north, 0), (south, 160)):
        @pl.when(jnp.logical_not(edge))
        def _():
            for k in range(3):
                ext[k, at:at + 32, :] = jnp.zeros((32, LANES), jnp.float32)

    for side in range(2):
        pltpu.make_async_copy(beside.at[side], beside.at[side], beside_recv.at[side]).wait()
        ext[2 * side, 32:160, :] = turned(beside.at[side])
        pltpu.make_async_copy(recv2, recv2, beside_send.at[side]).wait()
    for there, to in ((north, -1), (south, 1)):
        @pl.when(there)
        def _():
            for dd in (-1, 0, 1):
                near(dd, to).wait_send()
                near(dd, -to).wait_recv()

    @pl.when(owner)
    def _():
        for src, i in ((send1, 0), (send2, 2)):
            part = src.at[:, pl.ds(0, src.shape[1] - 2)]
            pltpu.make_async_copy(part, part, sems.at[i]).wait()

    @pl.when(jnp.logical_not(owner))
    def _():
        pltpu.make_async_copy(send1, send1, sems.at[0]).wait()


def memo(f):
    seen = {}

    def g(i):
        if i not in seen:
            seen[i] = f(i)
        return seen[i]

    return g


def v_cycle(load, c0, inside):
    lane = lane_iota(8)

    def coefs(c):
        diag = 1.0 + 4.0 * c
        beta = inside * (0.8 / diag)
        return diag, c * inside, beta, beta * c

    diag0, mult0, beta0, gamma0 = coefs(c0)
    diag1, mult1, beta1, gamma1 = coefs(c0 * 0.25)
    diag2, mult2, beta2, gamma2 = coefs(c0 * 0.0625)

    def pairs(x, step):
        def f(i):
            return (x(i - 1) + x(i + 1)) + (roll(x(i), step) + roll(x(i), -step))
        return f

    def second(first, gamma, step):
        s = pairs(first, step)
        return memo(lambda i: 1.2 * first(i) + gamma * s(i))

    def sweep(x, first, gamma, step):
        s = pairs(x, step)
        return memo(lambda i: (0.2 * x(i) + first(i)) + gamma * s(i))

    def defect(x, rhs, diag, mult, step):
        s = pairs(x, step)
        return memo(lambda i: (rhs(i) - diag * x(i)) + mult * s(i))

    def restrict(x, step):
        even = (lane // step) % 2 == 0

        def f(i):
            q = x(2 * i) + x(2 * i + 1)
            return 0.25 * (q + jnp.where(even, roll(q, -step), roll(q, step)))
        return memo(f)

    def all_of(f, low, high):
        for i in range(low, high + 1):
            f(i)
        return f

    dep = all_of(memo(load), -26, 57)
    first0 = all_of(memo(lambda i: beta0 * dep(i)), -26, 57)
    x0 = all_of(second(first0, gamma0, 1), -25, 56)
    rhs1 = all_of(restrict(all_of(defect(x0, dep, diag0, mult0, 1), -24, 55), 1), -12, 27)
    first1 = all_of(memo(lambda i: beta1 * rhs1(i)), -12, 27)
    x1 = all_of(second(first1, gamma1, 2), -11, 26)
    rhs2 = all_of(restrict(all_of(defect(x1, rhs1, diag1, mult1, 2), -10, 25), 2), -5, 12)
    first2 = all_of(memo(lambda i: beta2 * rhs2(i)), -5, 12)
    x2 = all_of(second(first2, gamma2, 4), -4, 11)
    x2 = all_of(sweep(x2, first2, gamma2, 4), -3, 10)
    x2 = all_of(sweep(x2, first2, gamma2, 4), -2, 9)
    y1 = all_of(memo(lambda i: x1(i) + x2(i >> 1)), -3, 18)
    y1 = all_of(sweep(y1, first1, gamma1, 2), -2, 17)
    y1 = all_of(sweep(y1, first1, gamma1, 2), -1, 16)
    y0 = all_of(memo(lambda i: x0(i) + y1(i >> 1)), -2, 33)
    y0 = all_of(sweep(y0, first0, gamma0, 1), -1, 32)
    return sweep(y0, first0, gamma0, 1)


def window(rows):
    lane = lane_iota(8)

    def load(i):
        k, hi, r = (i + 32) // 32, (i % 32) // 16, i % 16
        before, here, after = rows(k, r), rows(k, r + 32), rows(k, r + 64)
        if hi == 0:
            return jnp.where(lane < 64, here, roll(jnp.where(lane < 32, after, before), 64))
        return jnp.where(lane < 64, roll(here, 64), jnp.where(lane < 96, after, before))

    return load


def inside_of(g):
    chunk, lane = sub_iota() // 2, lane_iota(8)
    out = ((g == 0) & (chunk == 0) & (lane >= 96)) | ((g == NLATDEV - 1) & (chunk == 3) & (lane >= 64) & (lane < 96))
    return jnp.where(out, 0.0, 1.0)


def cycle_kernel(ext, coef, out, rows, block, sems):
    g = lax.axis_index("lat")
    result = v_cycle(window(lambda k, at: ext[k, pl.ds(at, 8, stride=16), :]), coef[...], inside_of(g))
    low = lane_iota(8) < 64
    copies = []
    for b in range(4):
        for i in range(8 * b, 8 * b + 8):
            rows[8 * i:8 * i + 8, :] = result(i)
        for lev in range(2):
            for pair in range(2):
                left = rows[pl.ds(64 * b + 4 * pair + lev, 8, stride=8), :]
                right = rows[pl.ds(64 * b + 4 * pair + 2 + lev, 8, stride=8), :]
                block[lev, 8 * b:8 * b + 8, 128 * pair:128 * pair + 128] = jnp.where(
                    low, left, roll(right, 64))
        part = (slice(None), pl.ds(8 * b, 8))
        copies.append(pltpu.make_async_copy(block.at[part], out.at[part], sems.at[b]))
        copies[-1].start()
    for copy in copies:
        copy.wait()


def per_device(field, offsets, fraction, helm):
    vmem = pl.BlockSpec(memory_space=pltpu.VMEM)
    hbm = pl.BlockSpec(memory_space=pltpu.HBM)
    parts = pltpu.VMEM((REP, 2 * OWNERS, LANES), jnp.float32)
    circles = pltpu.VMEM((REP, LANES, LANES), jnp.float32)
    inputs = [pltpu.with_memory_space_constraint(a, pltpu.HBM) for a in (field, offsets, fraction, helm)]
    ext, coef = pl.pallas_call(
        exchange_kernel,
        out_shape=(jax.ShapeDtypeStruct((3, 192, LANES), jnp.float32), jax.ShapeDtypeStruct((8, LANES), jnp.float32)),
        in_specs=[hbm] * 4,
        out_specs=(vmem, vmem),
        scratch_shapes=[
            pltpu.VMEM(field.shape, jnp.float32),
            pltpu.SMEM(offsets.shape, jnp.int32),
            pltpu.SMEM(fraction.shape, jnp.float32),
            pltpu.SMEM(helm.shape, jnp.float32),
            parts, circles, circles, parts, circles,
            pltpu.VMEM((2, REP, 2 * OWNERS, LANES), jnp.float32),
            pltpu.SemaphoreType.DMA((7,)),
            pltpu.SemaphoreType.DMA((3 + PLANES,)),
            pltpu.SemaphoreType.DMA((2,)),
            pltpu.SemaphoreType.DMA((2,)),
            pltpu.SemaphoreType.DMA((2, 3)),
            pltpu.SemaphoreType.DMA((2, 3)),
            pltpu.SemaphoreType.REGULAR,
            pltpu.SemaphoreType.REGULAR,
        ],
        compiler_params=pltpu.CompilerParams(collective_id=0, has_side_effects=True, vmem_limit_bytes=16 * 1024 * 1024),
    )(*inputs)
    return pl.pallas_call(
        cycle_kernel,
        out_shape=jax.ShapeDtypeStruct(field.shape, jnp.float32),
        in_specs=[vmem, vmem],
        out_specs=hbm,
        scratch_shapes=[
            pltpu.VMEM((256, LANES), jnp.float32),
            pltpu.VMEM(field.shape, jnp.float32),
            pltpu.SemaphoreType.DMA((4,)),
        ],
        compiler_params=pltpu.CompilerParams(vmem_limit_bytes=16 * 1024 * 1024),
    )(ext, coef)


def solution(mesh):
    return jax.shard_map(
        per_device,
        mesh=mesh,
        in_specs=(P(None, "lon", "lat"), P("lat"), P("lat"), P()),
        out_specs=P(None, "lon", "lat"),
        check_vma=False,
    )
```

```python
import jax
import jax.numpy as jnp
from jax import lax
from jax.experimental import pallas as pl
from jax.experimental.pallas import tpu as pltpu
from jax.sharding import PartitionSpec as P

MESH = pl.DeviceIdType.MESH
NLONDEV = 64
NLATDEV = 8
FIRST = 0
PLANES = 4
OWNERS = 4 * PLANES
REP = NLONDEV // OWNERS
SERVED = (15, 4, 0, 5, 1, 6, 2, 9, 3, 7, 8, 10, 11, 12, 13, 14)
SPLIT = PLANES + (16 - PLANES) // 2
LANES = 128


def roll(x, shift):
    return pltpu.roll(x, shift % LANES, 1)


def lane_iota(rows):
    return lax.broadcasted_iota(jnp.int32, (rows, LANES), 1)


def sub_iota():
    return lax.broadcasted_iota(jnp.int32, (8, LANES), 0)


def pack_field(half):
    low = lane_iota(16) < 64
    pieces = []
    for chunk in range(4):
        for lev in range(2):
            first, second = half(lev, 0, chunk // 2), half(lev, 1, chunk // 2)
            if chunk % 2 == 0:
                pieces.append(jnp.where(low, first, roll(second, 64)))
            else:
                pieces.append(jnp.where(low, roll(first, 64), second))
    return jnp.concatenate(pieces, axis=0)


def by_chunk(chunk, values, dtype):
    full = jnp.full((8, LANES), values[0], dtype)
    for c in range(1, 4):
        full = jnp.where(chunk == c, jnp.full((8, LANES), values[c], dtype), full)
    return full


def shift_coarse(x, offset):
    v = [x[8 * i:8 * i + 8] for i in range(16)]
    sub = sub_iota()
    for bit in range(7):
        by = 1 << bit
        take = (offset // (16 * by)) % 2 == 1
        if by < 8:
            turned = [pltpu.roll(u, by, 0) for u in v]
            moved = [jnp.where(sub < by, turned[i - 1], turned[i]) for i in range(16)]
        else:
            moved = [v[i - by // 8] for i in range(16)]
        v = [jnp.where(take, m, u) for m, u in zip(moved, v)]
    return jnp.concatenate(v, axis=0)


def shift_fine(v, offset):
    for bit in range(4):
        by = 1 << bit
        take = (offset // by) % 2 == 1
        v = [jnp.where(take, v[r - by] if r >= by else roll(v[r - by + 16], 1), v[r]) for r in range(16)]
    return v


def interpolate(g, s):
    w_one = -s * (s - 1.0) * (s - 2.0) / 6.0
    w_two = (s + 1.0) * (s - 1.0) * (s - 2.0) / 2.0
    w_three = -(s + 1.0) * s * (s - 2.0) / 2.0
    w_four = (s + 1.0) * s * (s - 1.0) / 6.0
    ext = [roll(g[14], 1), roll(g[15], 1)] + g + [roll(g[0], -1)]
    return [w_one * ext[r + 3] + w_two * ext[r + 2] + w_three * ext[r + 1] + w_four * ext[r] for r in range(16)]


def exchange_kernel(field_in, offsets_in, fraction_in, helm_in, ext, coef, field, offsets, fraction, helm, send1, recv1, send2, recv2, work,
                    beside,
                    load_sems, sems, beside_send, beside_recv, near_send, near_recv, lat_in, may_near):
    d = lax.axis_index("lon")
    g = lax.axis_index("lat")
    north, south = g > 0, g < NLATDEV - 1
    rank = lax.rem(d + NLONDEV - 4 * FIRST, NLONDEV)
    owner = rank < OWNERS

    parts = [(lev, pl.ds(16 * hi, 16)) for lev in range(2) for hi in range(2)]
    loads = [pltpu.make_async_copy(src, dst, load_sems.at[i]) for i, (src, dst) in enumerate(
        [(field_in.at[at], field.at[at]) for at in parts]
        + [(offsets_in, offsets), (fraction_in, fraction), (helm_in, helm)])]
    for load in loads:
        load.start()

    barrier = pltpu.get_barrier_semaphore()

    def tell_lat(sem):
        for there, to in ((north, -1), (south, 1)):
            @pl.when(there)
            def _():
                pl.semaphore_signal(sem, inc=1, device_id={"lat": g + to}, device_id_type=MESH)

    @pl.when(owner)
    def _():
        def greet(j, carry):
            to = lax.rem(OWNERS + 4 * FIRST + j, NLONDEV)

            @pl.when(to != d)
            def _():
                pl.semaphore_signal(barrier, inc=1, device_id={"lon": to}, device_id_type=MESH)
            return carry

        tell_lat(barrier)
        lax.fori_loop(0, NLONDEV, greet, 0)

    for load in loads[:4]:
        load.wait()
    packed = pack_field(lambda lev, hi, pair: field[lev, 16 * hi:16 * hi + 16, 128 * pair:128 * pair + 128]).T
    for hi in range(2):
        for s in range(REP):
            at = 64 * hi + OWNERS * s
            send1[s, pl.ds(hi, OWNERS, stride=2), :] = packed[at:at + OWNERS]

    one = owner.astype(jnp.int32)
    sides = north.astype(jnp.int32) + south.astype(jnp.int32)
    pl.semaphore_wait(barrier, OWNERS - one + one * sides)
    mine, ranked = pl.ds(2 * d, 2), pl.ds(2 * rank, 2)

    def collect(j, carry):
        k = j // 4
        farthest = 4 * jnp.where(d >= 40, PLANES - 1 - k, k) + lax.rem(j + d, 4)
        to_rank = jnp.where(owner, lax.rem(rank + j, OWNERS), farthest)
        to = lax.rem(to_rank + 4 * FIRST, NLONDEV)
        pltpu.make_async_remote_copy(
            src_ref=send1.at[:, pl.ds(2 * to_rank, 2)], dst_ref=recv1.at[:, mine],
            send_sem=sems.at[0], recv_sem=sems.at[1],
            device_id={"lon": to}, device_id_type=MESH,
        ).start()
        return carry

    lax.fori_loop(one, OWNERS, collect, 0)
    for load in loads[4:]:
        load.wait()
    coef[...] = jnp.where(sub_iota() % 2 == 0, jnp.full((8, LANES), helm[0], jnp.float32),
                          jnp.full((8, LANES), helm[1], jnp.float32))

    @pl.when(owner)
    def _():
        pltpu.make_async_copy(send1.at[:, ranked], recv1.at[:, mine], sems.at[1]).start()
        pltpu.make_async_copy(recv1, recv1, sems.at[1]).wait()
        tell_lat(lat_in)
        for s in range(REP):
            own = [rank + OWNERS * s + 64 * c for c in range(4)]
            turns = [offsets[i] for i in own]
            work[s] = shift_coarse(recv1[s], by_chunk(lane_iota(8) // 32, turns, jnp.int32)).T
            v = [work[s, pl.ds(r, 8, stride=16), :] for r in range(16)]
            v = shift_fine(v, by_chunk(sub_iota() // 2, turns, jnp.int32))
            v = interpolate(v, by_chunk(sub_iota() // 2, [fraction[i] for i in own], jnp.float32))
            for r in range(16):
                work[s, pl.ds(r, 8, stride=16), :] = v[r]
            send2[s] = work[s].T

        for plane in SERVED:
            def spread(j, carry):
                to = 4 * plane + lax.rem(j + d, 4)

                @pl.when(to != d)
                def _():
                    pltpu.make_async_remote_copy(
                        src_ref=send2.at[:, pl.ds(2 * to, 2)], dst_ref=recv2.at[:, ranked],
                        send_sem=sems.at[2], recv_sem=sems.at[3 + rank // 4],
                        device_id={"lon": to}, device_id_type=MESH,
                    ).start()
                return carry

            lax.fori_loop(0, 4, spread, 0)

        pltpu.make_async_copy(send2.at[:, mine], recv2.at[:, ranked], sems.at[3 + rank // 4]).start()
        pl.semaphore_wait(lat_in, sides)
        for i in range(OWNERS, NLONDEV, OWNERS):
            pl.semaphore_signal(may_near, inc=1, device_id={"lon": lax.rem(d + i, NLONDEV)}, device_id_type=MESH)

    falling = (rank >= OWNERS) & (rank < 4 * SPLIT)
    for k in range(PLANES):
        p = jnp.where(falling, PLANES - 1 - k, k)
        part = recv2.at[:, pl.ds(pl.multiple_of(8 * p, 8), 8)]
        pltpu.make_async_copy(part, part, sems.at[3 + p]).wait()
        for side, dd in ((0, 1), (1, -1)):
            pltpu.make_async_remote_copy(
                src_ref=part, dst_ref=beside.at[side, :, pl.ds(pl.multiple_of(8 * p, 8), 8)],
                send_sem=beside_send.at[side], recv_sem=beside_recv.at[side],
                device_id={"lon": lax.rem(d + dd + NLONDEV, NLONDEV)}, device_id_type=MESH,
            ).start()

    def turned(rows):
        return jnp.concatenate(
            [rows[s, pl.ds(hi, OWNERS, stride=2), :] for hi in range(2) for s in range(REP)], axis=0).T

    ext[1, 32:160, :] = turned(recv2)

    def near(dd, to):
        if to < 0:
            src, dst = ext.at[1, pl.ds(32, 32)], ext.at[1 - dd, pl.ds(160, 32)]
        else:
            src, dst = ext.at[1, pl.ds(128, 32)], ext.at[1 - dd, pl.ds(0, 32)]
        return pltpu.make_async_remote_copy(
            src_ref=src, dst_ref=dst,
            send_sem=near_send.at[(to + 1) // 2, dd + 1], recv_sem=near_recv.at[(to + 1) // 2, dd + 1],
            device_id={"lon": lax.rem(d + dd + NLONDEV, NLONDEV), "lat": g + to},
            device_id_type=MESH)

    @pl.when(jnp.logical_not(owner))
    def _():
        pl.semaphore_wait(may_near, 1)

    for there, to in ((north, -1), (south, 1)):
        @pl.when(there)
        def _():
            for dd in (-1, 0, 1):
                near(dd, to).start()
    for edge, at in ((north, 0), (south, 160)):
        @pl.when(jnp.logical_not(edge))
        def _():
            for k in range(3):
                ext[k, at:at + 32, :] = jnp.zeros((32, LANES), jnp.float32)

    for side in range(2):
        pltpu.make_async_copy(beside.at[side], beside.at[side], beside_recv.at[side]).wait()
        ext[2 * side, 32:160, :] = turned(beside.at[side])
        pltpu.make_async_copy(recv2, recv2, beside_send.at[side]).wait()
    for there, to in ((north, -1), (south, 1)):
        @pl.when(there)
        def _():
            for dd in (-1, 0, 1):
                near(dd, to).wait_send()
                near(dd, -to).wait_recv()

    @pl.when(owner)
    def _():
        for src, i in ((send1, 0), (send2, 2)):
            part = src.at[:, pl.ds(0, src.shape[1] - 2)]
            pltpu.make_async_copy(part, part, sems.at[i]).wait()

    @pl.when(jnp.logical_not(owner))
    def _():
        pltpu.make_async_copy(send1, send1, sems.at[0]).wait()


def memo(f):
    seen = {}

    def g(i):
        if i not in seen:
            seen[i] = f(i)
        return seen[i]

    return g


def v_cycle(load, c0, inside):
    lane = lane_iota(8)

    def coefs(c):
        diag = 1.0 + 4.0 * c
        beta = inside * (0.8 / diag)
        return diag, c * inside, beta, beta * c

    diag0, mult0, beta0, gamma0 = coefs(c0)
    diag1, mult1, beta1, gamma1 = coefs(c0 * 0.25)
    diag2, mult2, beta2, gamma2 = coefs(c0 * 0.0625)

    def pairs(x, step):
        def f(i):
            return (x(i - 1) + x(i + 1)) + (roll(x(i), step) + roll(x(i), -step))
        return f

    def second(first, gamma, step):
        s = pairs(first, step)
        return memo(lambda i: 1.2 * first(i) + gamma * s(i))

    def sweep(x, first, gamma, step):
        s = pairs(x, step)
        return memo(lambda i: (0.2 * x(i) + first(i)) + gamma * s(i))

    def defect(x, rhs, diag, mult, step):
        s = pairs(x, step)
        return memo(lambda i: (rhs(i) - diag * x(i)) + mult * s(i))

    def restrict(x, step):
        def f(i):
            q = x(2 * i) + x(2 * i + 1)
            return 0.25 * (q + roll(q, -step))
        return memo(f)

    def filled(x, step):
        first = (lane // step) % 2 == 0
        return memo(lambda i: jnp.where(first, x(i), roll(x(i), step)))

    def all_of(f, low, high):
        for i in range(low, high + 1):
            f(i)
        return f

    dep = all_of(memo(load), -26, 57)
    first0 = all_of(memo(lambda i: beta0 * dep(i)), -26, 57)
    x0 = all_of(second(first0, gamma0, 1), -25, 56)
    rhs1 = all_of(restrict(all_of(defect(x0, dep, diag0, mult0, 1), -24, 55), 1), -12, 27)
    first1 = all_of(memo(lambda i: beta1 * rhs1(i)), -12, 27)
    x1 = all_of(second(first1, gamma1, 2), -11, 26)
    rhs2 = all_of(restrict(all_of(defect(x1, rhs1, diag1, mult1, 2), -10, 25), 2), -5, 12)
    first2 = all_of(memo(lambda i: beta2 * rhs2(i)), -5, 12)
    x2 = all_of(second(first2, gamma2, 4), -4, 11)
    x2 = all_of(sweep(x2, first2, gamma2, 4), -3, 10)
    x2 = all_of(sweep(x2, first2, gamma2, 4), -2, 9)
    fill2 = all_of(filled(x2, 2), -2, 9)
    y1 = all_of(memo(lambda i: x1(i) + fill2(i >> 1)), -3, 18)
    y1 = all_of(sweep(y1, first1, gamma1, 2), -2, 17)
    y1 = all_of(sweep(y1, first1, gamma1, 2), -1, 16)
    fill1 = all_of(filled(y1, 1), -1, 16)
    y0 = all_of(memo(lambda i: x0(i) + fill1(i >> 1)), -2, 33)
    y0 = all_of(sweep(y0, first0, gamma0, 1), -1, 32)
    return sweep(y0, first0, gamma0, 1)


def window(rows):
    lane = lane_iota(8)

    def load(i):
        k, hi, r = (i + 32) // 32, (i % 32) // 16, i % 16
        before, here, after = rows(k, r), rows(k, r + 32), rows(k, r + 64)
        if hi == 0:
            return jnp.where(lane < 64, here, roll(jnp.where(lane < 32, after, before), 64))
        return jnp.where(lane < 64, roll(here, 64), jnp.where(lane < 96, after, before))

    return load


def inside_of(g):
    chunk, lane = sub_iota() // 2, lane_iota(8)
    out = ((g == 0) & (chunk == 0) & (lane >= 96)) | ((g == NLATDEV - 1) & (chunk == 3) & (lane >= 64) & (lane < 96))
    return jnp.where(out, 0.0, 1.0)


def cycle_kernel(ext, coef, out, rows, block, sems):
    g = lax.axis_index("lat")
    result = v_cycle(window(lambda k, at: ext[k, pl.ds(at, 8, stride=16), :]), coef[...], inside_of(g))
    low = lane_iota(8) < 64
    copies = []
    for b in range(4):
        for i in range(8 * b, 8 * b + 8):
            rows[8 * i:8 * i + 8, :] = result(i)
        for lev in range(2):
            for pair in range(2):
                left = rows[pl.ds(64 * b + 4 * pair + lev, 8, stride=8), :]
                right = rows[pl.ds(64 * b + 4 * pair + 2 + lev, 8, stride=8), :]
                block[lev, 8 * b:8 * b + 8, 128 * pair:128 * pair + 128] = jnp.where(
                    low, left, roll(right, 64))
        part = (slice(None), pl.ds(8 * b, 8))
        copies.append(pltpu.make_async_copy(block.at[part], out.at[part], sems.at[b]))
        copies[-1].start()
    for copy in copies:
        copy.wait()


def per_device(field, offsets, fraction, helm):
    vmem = pl.BlockSpec(memory_space=pltpu.VMEM)
    hbm = pl.BlockSpec(memory_space=pltpu.HBM)
    parts = pltpu.VMEM((REP, 2 * OWNERS, LANES), jnp.float32)
    circles = pltpu.VMEM((REP, LANES, LANES), jnp.float32)
    inputs = [pltpu.with_memory_space_constraint(a, pltpu.HBM) for a in (field, offsets, fraction, helm)]
    ext, coef = pl.pallas_call(
        exchange_kernel,
        out_shape=(jax.ShapeDtypeStruct((3, 192, LANES), jnp.float32), jax.ShapeDtypeStruct((8, LANES), jnp.float32)),
        in_specs=[hbm] * 4,
        out_specs=(vmem, vmem),
        scratch_shapes=[
            pltpu.VMEM(field.shape, jnp.float32),
            pltpu.SMEM(offsets.shape, jnp.int32),
            pltpu.SMEM(fraction.shape, jnp.float32),
            pltpu.SMEM(helm.shape, jnp.float32),
            parts, circles, circles, parts, circles,
            pltpu.VMEM((2, REP, 2 * OWNERS, LANES), jnp.float32),
            pltpu.SemaphoreType.DMA((7,)),
            pltpu.SemaphoreType.DMA((3 + PLANES,)),
            pltpu.SemaphoreType.DMA((2,)),
            pltpu.SemaphoreType.DMA((2,)),
            pltpu.SemaphoreType.DMA((2, 3)),
            pltpu.SemaphoreType.DMA((2, 3)),
            pltpu.SemaphoreType.REGULAR,
            pltpu.SemaphoreType.REGULAR,
        ],
        compiler_params=pltpu.CompilerParams(collective_id=0, has_side_effects=True, vmem_limit_bytes=16 * 1024 * 1024),
    )(*inputs)
    return pl.pallas_call(
        cycle_kernel,
        out_shape=jax.ShapeDtypeStruct(field.shape, jnp.float32),
        in_specs=[vmem, vmem],
        out_specs=hbm,
        scratch_shapes=[
            pltpu.VMEM((256, LANES), jnp.float32),
            pltpu.VMEM(field.shape, jnp.float32),
            pltpu.SemaphoreType.DMA((4,)),
        ],
        compiler_params=pltpu.CompilerParams(vmem_limit_bytes=16 * 1024 * 1024),
    )(ext, coef)


def solution(mesh):
    return jax.shard_map(
        per_device,
        mesh=mesh,
        in_specs=(P(None, "lon", "lat"), P("lat"), P("lat"), P()),
        out_specs=P(None, "lon", "lat"),
        check_vma=False,
    )
```

```python
import jax
import jax.numpy as jnp
from jax import lax
from jax.experimental import pallas as pl
from jax.experimental.pallas import tpu as pltpu
from jax.sharding import PartitionSpec as P

MESH = pl.DeviceIdType.MESH
NLONDEV = 64
NLATDEV = 8
FIRST = 0
PLANES = 4
OWNERS = 4 * PLANES
REP = NLONDEV // OWNERS
SERVED = (15, 4, 0, 5, 1, 6, 2, 9, 3, 7, 8, 10, 11, 12, 13, 14)
SPLIT = PLANES + (16 - PLANES) // 2
LANES = 128


def roll(x, shift):
    return pltpu.roll(x, shift % LANES, 1)


def lane_iota(rows):
    return lax.broadcasted_iota(jnp.int32, (rows, LANES), 1)


def sub_iota():
    return lax.broadcasted_iota(jnp.int32, (8, LANES), 0)


def pack_field(half):
    low = lane_iota(16) < 64
    pieces = []
    for chunk in range(4):
        for lev in range(2):
            first, second = half(lev, 0, chunk // 2), half(lev, 1, chunk // 2)
            if chunk % 2 == 0:
                pieces.append(jnp.where(low, first, roll(second, 64)))
            else:
                pieces.append(jnp.where(low, roll(first, 64), second))
    return jnp.concatenate(pieces, axis=0)


def by_chunk(chunk, values, dtype):
    full = jnp.full((8, LANES), values[0], dtype)
    for c in range(1, 4):
        full = jnp.where(chunk == c, jnp.full((8, LANES), values[c], dtype), full)
    return full


def shift_coarse(x, offset):
    v = [x[8 * i:8 * i + 8] for i in range(16)]
    sub = sub_iota()
    for bit in range(7):
        by = 1 << bit
        take = (offset // (16 * by)) % 2 == 1
        if by < 8:
            turned = [pltpu.roll(u, by, 0) for u in v]
            moved = [jnp.where(sub < by, turned[i - 1], turned[i]) for i in range(16)]
        else:
            moved = [v[i - by // 8] for i in range(16)]
        v = [jnp.where(take, m, u) for m, u in zip(moved, v)]
    return jnp.concatenate(v, axis=0)


def shift_fine(v, offset):
    for bit in range(4):
        by = 1 << bit
        take = (offset // by) % 2 == 1
        v = [jnp.where(take, v[r - by] if r >= by else roll(v[r - by + 16], 1), v[r]) for r in range(16)]
    return v


def interpolate(g, s):
    w_one = -s * (s - 1.0) * (s - 2.0) / 6.0
    w_two = (s + 1.0) * (s - 1.0) * (s - 2.0) / 2.0
    w_three = -(s + 1.0) * s * (s - 2.0) / 2.0
    w_four = (s + 1.0) * s * (s - 1.0) / 6.0
    ext = [roll(g[14], 1), roll(g[15], 1)] + g + [roll(g[0], -1)]
    return [w_one * ext[r + 3] + w_two * ext[r + 2] + w_three * ext[r + 1] + w_four * ext[r] for r in range(16)]


def exchange_kernel(field_in, offsets_in, fraction_in, helm_in, ext, coef, field, offsets, fraction, helm, send1, recv1, send2, recv2, work,
                    beside,
                    load_sems, sems, beside_send, beside_recv, near_send, near_recv, lat_in, may_near):
    d = lax.axis_index("lon")
    g = lax.axis_index("lat")
    north, south = g > 0, g < NLATDEV - 1
    rank = lax.rem(d + NLONDEV - 4 * FIRST, NLONDEV)
    owner = rank < OWNERS

    parts = [(lev, pl.ds(16 * hi, 16)) for lev in range(2) for hi in range(2)]
    loads = [pltpu.make_async_copy(src, dst, load_sems.at[i]) for i, (src, dst) in enumerate(
        [(field_in.at[at], field.at[at]) for at in parts]
        + [(offsets_in, offsets), (fraction_in, fraction), (helm_in, helm)])]
    for load in loads:
        load.start()

    barrier = pltpu.get_barrier_semaphore()

    def tell_lat(sem):
        for there, to in ((north, -1), (south, 1)):
            @pl.when(there)
            def _():
                pl.semaphore_signal(sem, inc=1, device_id={"lat": g + to}, device_id_type=MESH)

    @pl.when(owner)
    def _():
        def greet(j, carry):
            to = lax.rem(OWNERS + 4 * FIRST + j, NLONDEV)

            @pl.when(to != d)
            def _():
                pl.semaphore_signal(barrier, inc=1, device_id={"lon": to}, device_id_type=MESH)
            return carry

        tell_lat(barrier)
        lax.fori_loop(0, NLONDEV, greet, 0)

    for load in loads[:4]:
        load.wait()
    packed = pack_field(lambda lev, hi, pair: field[lev, 16 * hi:16 * hi + 16, 128 * pair:128 * pair + 128]).T
    for hi in range(2):
        for s in range(REP):
            at = 64 * hi + OWNERS * s
            send1[s, pl.ds(hi, OWNERS, stride=2), :] = packed[at:at + OWNERS]

    one = owner.astype(jnp.int32)
    sides = north.astype(jnp.int32) + south.astype(jnp.int32)
    pl.semaphore_wait(barrier, OWNERS - one + one * sides)
    mine, ranked = pl.ds(2 * d, 2), pl.ds(2 * rank, 2)

    def block(ref, i):
        return ref.at[pl.ds(pl.multiple_of(8 * i, 8), 8)]


    def collect(j, carry):
        k = j // 4
        farthest = 4 * jnp.where(d >= 40, PLANES - 1 - k, k) + lax.rem(j + d, 4)
        to_rank = jnp.where(owner, lax.rem(rank + j, OWNERS), farthest)
        to = lax.rem(to_rank + 4 * FIRST, NLONDEV)
        pltpu.make_async_remote_copy(
            src_ref=send1.at[:, pl.ds(2 * to_rank, 2)], dst_ref=recv1.at[:, mine],
            send_sem=sems.at[0], recv_sem=sems.at[1],
            device_id={"lon": to}, device_id_type=MESH,
        ).start()
        return carry

    lax.fori_loop(one, OWNERS, collect, 0)
    for load in loads[4:]:
        load.wait()
    coef[...] = jnp.where(sub_iota() % 2 == 0, jnp.full((8, LANES), helm[0], jnp.float32),
                          jnp.full((8, LANES), helm[1], jnp.float32))

    @pl.when(owner)
    def _():
        pltpu.make_async_copy(send1.at[:, ranked], recv1.at[:, mine], sems.at[1]).start()
        pltpu.make_async_copy(recv1, recv1, sems.at[1]).wait()
        tell_lat(lat_in)
        for s in range(REP):
            own = [rank + OWNERS * s + 64 * c for c in range(4)]
            turns = [offsets[i] for i in own]
            work[s] = shift_coarse(recv1[s], by_chunk(lane_iota(8) // 32, turns, jnp.int32)).T
            v = [work[s, pl.ds(r, 8, stride=16), :] for r in range(16)]
            v = shift_fine(v, by_chunk(sub_iota() // 2, turns, jnp.int32))
            v = interpolate(v, by_chunk(sub_iota() // 2, [fraction[i] for i in own], jnp.float32))
            for r in range(16):
                work[s, pl.ds(r, 8, stride=16), :] = v[r]
            work[s] = work[s].T
            for hi in range(2):
                send2[pl.ds(2 * s + hi, 64, stride=8), :] = work[s, pl.ds(hi, 64, stride=2), :]

        for plane in SERVED:
            def spread(j, carry):
                to = 4 * plane + lax.rem(j + d, 4)

                @pl.when(to != d)
                def _():
                    pltpu.make_async_remote_copy(
                        src_ref=block(send2, to), dst_ref=block(recv2, rank),
                        send_sem=sems.at[2], recv_sem=sems.at[3 + rank // 4],
                        device_id={"lon": to}, device_id_type=MESH,
                    ).start()
                return carry

            lax.fori_loop(0, 4, spread, 0)

        pltpu.make_async_copy(block(send2, d), block(recv2, rank), sems.at[3 + rank // 4]).start()
        pl.semaphore_wait(lat_in, sides)
        for i in range(OWNERS, NLONDEV, OWNERS):
            pl.semaphore_signal(may_near, inc=1, device_id={"lon": lax.rem(d + i, NLONDEV)}, device_id_type=MESH)

    falling = (rank >= OWNERS) & (rank < 4 * SPLIT)
    for k in range(PLANES):
        p = jnp.where(falling, PLANES - 1 - k, k)
        rows = pl.ds(pl.multiple_of(32 * p, 32), 32)
        part = recv2.at[rows]
        pltpu.make_async_copy(part, part, sems.at[3 + p]).wait()
        for side, dd in ((0, 1), (1, -1)):
            pltpu.make_async_remote_copy(
                src_ref=part, dst_ref=beside.at[side, rows],
                send_sem=beside_send.at[side], recv_sem=beside_recv.at[side],
                device_id={"lon": lax.rem(d + dd + NLONDEV, NLONDEV)}, device_id_type=MESH,
            ).start()

    def turned(rows):
        return jnp.concatenate(
            [rows[pl.ds(2 * s + hi, OWNERS, stride=8), :] for hi in range(2) for s in range(REP)], axis=0).T

    ext[1, 32:160, :] = turned(recv2)

    def near(dd, to):
        if to < 0:
            src, dst = ext.at[1, pl.ds(32, 32)], ext.at[1 - dd, pl.ds(160, 32)]
        else:
            src, dst = ext.at[1, pl.ds(128, 32)], ext.at[1 - dd, pl.ds(0, 32)]
        return pltpu.make_async_remote_copy(
            src_ref=src, dst_ref=dst,
            send_sem=near_send.at[(to + 1) // 2, dd + 1], recv_sem=near_recv.at[(to + 1) // 2, dd + 1],
            device_id={"lon": lax.rem(d + dd + NLONDEV, NLONDEV), "lat": g + to},
            device_id_type=MESH)

    @pl.when(jnp.logical_not(owner))
    def _():
        pl.semaphore_wait(may_near, 1)

    for there, to in ((north, -1), (south, 1)):
        @pl.when(there)
        def _():
            for dd in (-1, 0, 1):
                near(dd, to).start()
    for edge, at in ((north, 0), (south, 160)):
        @pl.when(jnp.logical_not(edge))
        def _():
            for k in range(3):
                ext[k, at:at + 32, :] = jnp.zeros((32, LANES), jnp.float32)

    for side in range(2):
        pltpu.make_async_copy(beside.at[side], beside.at[side], beside_recv.at[side]).wait()
        ext[2 * side, 32:160, :] = turned(beside.at[side])
        pltpu.make_async_copy(recv2, recv2, beside_send.at[side]).wait()
    for there, to in ((north, -1), (south, 1)):
        @pl.when(there)
        def _():
            for dd in (-1, 0, 1):
                near(dd, to).wait_send()
                near(dd, -to).wait_recv()

    @pl.when(owner)
    def _():
        for part, i in ((send1.at[:, pl.ds(0, 2 * OWNERS - 2)], 0), (send2.at[pl.ds(0, 8 * NLONDEV - 8)], 2)):
            pltpu.make_async_copy(part, part, sems.at[i]).wait()

    @pl.when(jnp.logical_not(owner))
    def _():
        pltpu.make_async_copy(send1, send1, sems.at[0]).wait()


def memo(f):
    seen = {}

    def g(i):
        if i not in seen:
            seen[i] = f(i)
        return seen[i]

    return g


def v_cycle(load, c0, inside):
    lane = lane_iota(8)

    def coefs(c):
        diag = 1.0 + 4.0 * c
        beta = inside * (0.8 / diag)
        return diag, c * inside, beta, beta * c

    diag0, mult0, beta0, gamma0 = coefs(c0)
    diag1, mult1, beta1, gamma1 = coefs(c0 * 0.25)
    diag2, mult2, beta2, gamma2 = coefs(c0 * 0.0625)

    def pairs(x, step):
        def f(i):
            return (x(i - 1) + x(i + 1)) + (roll(x(i), step) + roll(x(i), -step))
        return f

    def second(first, gamma, step):
        s = pairs(first, step)
        return memo(lambda i: 1.2 * first(i) + gamma * s(i))

    def sweep(x, first, gamma, step):
        s = pairs(x, step)
        return memo(lambda i: (0.2 * x(i) + first(i)) + gamma * s(i))

    def defect(x, rhs, diag, mult, step):
        s = pairs(x, step)
        return memo(lambda i: (rhs(i) - diag * x(i)) + mult * s(i))

    def restrict(x, step):
        even = (lane // step) % 2 == 0

        def f(i):
            q = x(2 * i) + x(2 * i + 1)
            return 0.25 * (q + jnp.where(even, roll(q, -step), roll(q, step)))
        return memo(f)

    def all_of(f, low, high):
        for i in range(low, high + 1):
            f(i)
        return f

    dep = all_of(memo(load), -26, 57)
    first0 = all_of(memo(lambda i: beta0 * dep(i)), -26, 57)
    x0 = all_of(second(first0, gamma0, 1), -25, 56)
    rhs1 = all_of(restrict(all_of(defect(x0, dep, diag0, mult0, 1), -24, 55), 1), -12, 27)
    first1 = all_of(memo(lambda i: beta1 * rhs1(i)), -12, 27)
    x1 = all_of(second(first1, gamma1, 2), -11, 26)
    rhs2 = all_of(restrict(all_of(defect(x1, rhs1, diag1, mult1, 2), -10, 25), 2), -5, 12)
    first2 = all_of(memo(lambda i: beta2 * rhs2(i)), -5, 12)
    x2 = all_of(second(first2, gamma2, 4), -4, 11)
    x2 = all_of(sweep(x2, first2, gamma2, 4), -3, 10)
    x2 = all_of(sweep(x2, first2, gamma2, 4), -2, 9)
    y1 = all_of(memo(lambda i: x1(i) + x2(i >> 1)), -3, 18)
    y1 = all_of(sweep(y1, first1, gamma1, 2), -2, 17)
    y1 = all_of(sweep(y1, first1, gamma1, 2), -1, 16)
    y0 = all_of(memo(lambda i: x0(i) + y1(i >> 1)), -2, 33)
    y0 = all_of(sweep(y0, first0, gamma0, 1), -1, 32)
    return sweep(y0, first0, gamma0, 1)


def window(rows):
    lane = lane_iota(8)

    def load(i):
        k, hi, r = (i + 32) // 32, (i % 32) // 16, i % 16
        before, here, after = rows(k, r), rows(k, r + 32), rows(k, r + 64)
        if hi == 0:
            return jnp.where(lane < 64, here, roll(jnp.where(lane < 32, after, before), 64))
        return jnp.where(lane < 64, roll(here, 64), jnp.where(lane < 96, after, before))

    return load


def inside_of(g):
    chunk, lane = sub_iota() // 2, lane_iota(8)
    out = ((g == 0) & (chunk == 0) & (lane >= 96)) | ((g == NLATDEV - 1) & (chunk == 3) & (lane >= 64) & (lane < 96))
    return jnp.where(out, 0.0, 1.0)


def cycle_kernel(ext, coef, out, rows, block, sems):
    g = lax.axis_index("lat")
    result = v_cycle(window(lambda k, at: ext[k, pl.ds(at, 8, stride=16), :]), coef[...], inside_of(g))
    low = lane_iota(8) < 64
    copies = []
    for b in range(4):
        for i in range(8 * b, 8 * b + 8):
            rows[8 * i:8 * i + 8, :] = result(i)
        for lev in range(2):
            for pair in range(2):
                left = rows[pl.ds(64 * b + 4 * pair + lev, 8, stride=8), :]
                right = rows[pl.ds(64 * b + 4 * pair + 2 + lev, 8, stride=8), :]
                block[lev, 8 * b:8 * b + 8, 128 * pair:128 * pair + 128] = jnp.where(
                    low, left, roll(right, 64))
        part = (slice(None), pl.ds(8 * b, 8))
        copies.append(pltpu.make_async_copy(block.at[part], out.at[part], sems.at[b]))
        copies[-1].start()
    for copy in copies:
        copy.wait()


def per_device(field, offsets, fraction, helm):
    vmem = pl.BlockSpec(memory_space=pltpu.VMEM)
    hbm = pl.BlockSpec(memory_space=pltpu.HBM)
    parts = pltpu.VMEM((REP, 2 * OWNERS, LANES), jnp.float32)
    square = pltpu.VMEM((LANES, LANES), jnp.float32)
    circles = pltpu.VMEM((REP, LANES, LANES), jnp.float32)
    inputs = [pltpu.with_memory_space_constraint(a, pltpu.HBM) for a in (field, offsets, fraction, helm)]
    ext, coef = pl.pallas_call(
        exchange_kernel,
        out_shape=(jax.ShapeDtypeStruct((3, 192, LANES), jnp.float32), jax.ShapeDtypeStruct((8, LANES), jnp.float32)),
        in_specs=[hbm] * 4,
        out_specs=(vmem, vmem),
        scratch_shapes=[
            pltpu.VMEM(field.shape, jnp.float32),
            pltpu.SMEM(offsets.shape, jnp.int32),
            pltpu.SMEM(fraction.shape, jnp.float32),
            pltpu.SMEM(helm.shape, jnp.float32),
            parts, circles, pltpu.VMEM((8 * NLONDEV, LANES), jnp.float32), square, circles,
            pltpu.VMEM((2, LANES, LANES), jnp.float32),
            pltpu.SemaphoreType.DMA((7,)),
            pltpu.SemaphoreType.DMA((3 + PLANES,)),
            pltpu.SemaphoreType.DMA((2,)),
            pltpu.SemaphoreType.DMA((2,)),
            pltpu.SemaphoreType.DMA((2, 3)),
            pltpu.SemaphoreType.DMA((2, 3)),
            pltpu.SemaphoreType.REGULAR,
            pltpu.SemaphoreType.REGULAR,
        ],
        compiler_params=pltpu.CompilerParams(collective_id=0, has_side_effects=True, vmem_limit_bytes=16 * 1024 * 1024),
    )(*inputs)
    return pl.pallas_call(
        cycle_kernel,
        out_shape=jax.ShapeDtypeStruct(field.shape, jnp.float32),
        in_specs=[vmem, vmem],
        out_specs=hbm,
        scratch_shapes=[
            pltpu.VMEM((256, LANES), jnp.float32),
            pltpu.VMEM(field.shape, jnp.float32),
            pltpu.SemaphoreType.DMA((4,)),
        ],
        compiler_params=pltpu.CompilerParams(vmem_limit_bytes=16 * 1024 * 1024),
    )(ext, coef)


def solution(mesh):
    return jax.shard_map(
        per_device,
        mesh=mesh,
        in_specs=(P(None, "lon", "lat"), P("lat"), P("lat"), P()),
        out_specs=P(None, "lon", "lat"),
        check_vma=False,
    )
```
